128 devices in a mesh: blk: 16 (over x_hi, z, core), group: 8 (over y, x_lo).
Axes of the slice: x: 4 (x_hi: 2, x_lo: 2; x = x_hi * 2 + x_lo), y: 4, z: 4, core: 2. Of those that a mesh axis runs over, the one named last changes fastest.
Arguments:
- queries: bfloat16 [65536, 4096], P(('blk', 'group'))
- passages: bfloat16 [8192, 4096], P(('blk', 'group'))
- positives: int32 [65536], P(('blk', 'group')), may hold values from 0 to 1023
- hard_ids: int32 [65536, 8], P(('blk', 'group')), may hold values from 0 to 8191, as said below
Outputs:
- query_grads: bfloat16 [65536, 4096], P(('blk', 'group'))
- passage_grads: bfloat16 [8192, 4096], P(('blk', 'group'))
- losses: float32 [65536], P(('blk', 'group'))
The draws below stay inside these ranges and needn't reach their ends.
Inputs may be any that keep to these rules, and one draw needn't show every extreme that they name: `hard_ids`: ids are passage rows. The 8 ids of a query are distinct. Among the queries of one aligned block of 512 query rows, at most 4 distinct ids fall in any aligned block of 64 passage rows, and exactly 4 in some such block.
All inputs are finite; a program needn't handle non-finite values.
Results may differ from the reference program's by a relative error of at most 0.02.
Values may be sent and summed in bfloat16 or wider, within the bound.
A program may use at most 128 MiB of HBM per device.

```python
import math
import jax
import jax.numpy as jnp
from jax import lax

D = 4096
Q_DEV = 512
P_DEV = 64
HARD = 8
CAP = 4
QUERIES = 65536
PASSAGES = 8192
CYCLE = 1024
N_BLK = 16
N_GROUP = 8


def rough_noise(key, shape):
    key_normal = jax.random.fold_in(key, 0)
    normal_part = jax.random.normal(key_normal, shape, jnp.float32)
    return normal_part


def passage_base(key):
    key = jax.random.fold_in(key, 11)
    key_center, key_assign, key_mixing, key_noise = jax.random.split(key, 4)
    groups = PASSAGES // CYCLE
    clusters = max(CYCLE // 8, 1)
    centers = rough_noise(key_center, (groups * clusters, D))
    row_ids = jnp.arange(PASSAGES, dtype=jnp.int32)
    owner_group = row_ids // P_DEV % groups
    cluster_ids = owner_group * clusters + jax.random.randint(key_assign, (PASSAGES,), 0, clusters)
    mixing = jnp.sqrt(jax.random.uniform(key_mixing, (PASSAGES, 1), jnp.float32, 0.6, 0.95))
    return mixing * centers[cluster_ids] + jnp.sqrt(1.0 - mixing * mixing) * rough_noise(key_noise, (PASSAGES, D))


def all_positives(key):
    return jax.random.randint(jax.random.fold_in(key, 17), (QUERIES,), 0, CYCLE).astype(jnp.int32)


def all_hard(key):
    key = jax.random.fold_in(key, 7)
    devices_all = QUERIES // Q_DEV
    slots = devices_all * CAP

    def one_device(device_key):
        key_count, key_local, key_order, key_full = jax.random.split(device_key, 4)
        counts = jax.random.randint(key_count, (devices_all,), 1, CAP + 1)
        fullest = jax.random.randint(key_full, (), 0, devices_all)
        counts = jnp.where(jnp.arange(devices_all) == fullest, CAP, counts)
        local_ids = jax.vmap(lambda owner_key: jax.random.permutation(owner_key, P_DEV)[:CAP])(jax.random.split(key_local, devices_all))
        table = (jnp.arange(devices_all)[:, None] * P_DEV + local_ids).reshape(-1)
        usable = (jnp.arange(CAP)[None, :] < counts[:, None]).reshape(-1)
        shuffle = jax.random.permutation(key_order, slots)
        order = jnp.argsort(jnp.where(usable, 0, slots) + shuffle)
        listing = table[order]
        usable_count = jnp.sum(usable.astype(jnp.int32))
        position = jnp.arange(Q_DEV * HARD) % usable_count
        return listing[position].reshape(Q_DEV, HARD).astype(jnp.int32)
    return jax.vmap(one_device)(jax.random.split(key, devices_all)).reshape(QUERIES, HARD)


def query_directions(key, base):
    positive_all = all_positives(key)
    hard_all = all_hard(key)
    key = jax.random.fold_in(key, 3)
    groups = PASSAGES // CYCLE
    devices_all = QUERIES // Q_DEV

    def one_block(block_index):
        block_key = jax.random.fold_in(key, block_index)
        key_weight, key_noise = jax.random.split(block_key)
        first_row = block_index * Q_DEV
        block_positive = lax.dynamic_slice_in_dim(positive_all, first_row, Q_DEV)
        block_hard = lax.dynamic_slice_in_dim(hard_all, first_row, Q_DEV)
        group_index = block_index % groups
        positive_rows = (block_positive // P_DEV * groups + group_index) * P_DEV + block_positive % P_DEV
        weights = jax.random.uniform(key_weight, (Q_DEV, HARD), jnp.float32, 0.5, 1.0)
        summed = base[positive_rows] + 0.5 * rough_noise(key_noise, (Q_DEV, D))
        for column in range(HARD):
            summed = summed + weights[:, column:column + 1] * base[block_hard[:, column]]
        return summed / 2.4
    return lax.map(one_block, jnp.arange(devices_all, dtype=jnp.int32)).reshape(QUERIES, D)


def draw_queries(key, part):
    directions = query_directions(key, passage_base(key))
    top_scale = 10.0
    key = jax.random.fold_in(key, 9)
    scales = jnp.exp(jax.random.uniform(key, (QUERIES, 1), jnp.float32, 0.0, math.log(top_scale)))
    return (scales * directions / math.sqrt(D)).astype(jnp.bfloat16)


def draw_passages(key, part):
    directions = passage_base(key)
    top_scale = 10.0
    key = jax.random.fold_in(key, 5)
    scales = jnp.exp(jax.random.uniform(key, (PASSAGES, 1), jnp.float32, 0.0, math.log(top_scale)))
    return (scales * directions / math.sqrt(D)).astype(jnp.bfloat16)


def draw_positives(key, part):
    return all_positives(key)


def draw_hard_ids(key, part):
    return all_hard(key)


def setup_inputs(seed: int = 0) -> dict:
    seeds = jax.random.split(jax.random.key(seed), 5)
    queries = draw_queries(jax.random.fold_in(seeds[4], 71), 0)
    passages = draw_passages(jax.random.fold_in(seeds[4], 71), 0)
    positives = draw_positives(jax.random.fold_in(seeds[4], 71), 0)
    hard_ids = draw_hard_ids(jax.random.fold_in(seeds[4], 71), 0)
    return dict(queries=queries, passages=passages, positives=positives, hard_ids=hard_ids)


logit_scale = 20.0
tiny_eps = 1e-06

def unit_rows(matrix):
    values = matrix.astype(jnp.float32)
    norms = jnp.sqrt(lax.optimization_barrier(jnp.sum(values * values, axis=-1, keepdims=True)) + tiny_eps)
    return (values / norms, norms)

def reference(queries, passages, positives, hard_ids):
    devices_all = N_BLK * N_GROUP
    feature_dim = queries.shape[1]
    passage_unit, passage_norm = unit_rows(passages)
    passage_hat = passage_unit.astype(jnp.bfloat16)

    def device_step(accum, inputs):
        index, block_queries, block_positives, block_ids = inputs
        group_index = index % N_GROUP
        cycle_index = ((jnp.arange(N_BLK, dtype=jnp.int32)[:, None] * N_GROUP + group_index) * P_DEV + jnp.arange(P_DEV, dtype=jnp.int32)[None, :]).reshape(-1).astype(jnp.int32)
        cycle_hat = passage_hat[cycle_index]
        query_unit, query_norm = unit_rows(block_queries)
        query_hat = query_unit.astype(jnp.bfloat16)
        cycle_scores = logit_scale * jnp.dot(query_hat, cycle_hat.T, preferred_element_type=jnp.float32)
        hard_hat = passage_hat[block_ids]
        hard_scores = logit_scale * jnp.einsum('qd,qhd->qh', query_hat.astype(jnp.float32), hard_hat.astype(jnp.float32))
        positive_score = jnp.take_along_axis(cycle_scores, block_positives[:, None], axis=1)[:, 0]
        cycle_lse = jnp.log(lax.optimization_barrier(jnp.sum(jnp.exp(cycle_scores), axis=1)))
        hard_lse = jnp.log(jnp.exp(positive_score) + lax.optimization_barrier(jnp.sum(jnp.exp(hard_scores), axis=1)))
        losses = cycle_lse + hard_lse - 2.0 * positive_score
        positive_weight = jnp.exp(positive_score - hard_lse)
        hard_weight = jnp.exp(hard_scores - hard_lse[:, None]).astype(jnp.bfloat16)
        onehot = jnp.arange(N_BLK * P_DEV, dtype=jnp.int32)[None, :] == block_positives[:, None]
        cycle_weight = (jnp.exp(cycle_scores - cycle_lse[:, None]) - jnp.where(onehot, (2.0 - positive_weight)[:, None], 0.0)).astype(jnp.bfloat16)
        query_sum = logit_scale * (jnp.dot(cycle_weight, cycle_hat, preferred_element_type=jnp.float32) + jnp.einsum('qh,qhd->qd', hard_weight.astype(jnp.float32), hard_hat.astype(jnp.float32)))
        query_grads = ((query_sum - query_unit * lax.optimization_barrier(jnp.sum(query_unit * query_sum, axis=1, keepdims=True))) / query_norm).astype(jnp.bfloat16)
        cycle_part = (logit_scale * jnp.dot(cycle_weight.T, query_hat, preferred_element_type=jnp.float32)).astype(jnp.bfloat16)
        accum = accum.at[cycle_index].add(cycle_part.astype(jnp.float32))
        flat_ids = block_ids.reshape(-1)
        distinct = jnp.unique(flat_ids, size=devices_all * CAP, fill_value=PASSAGES).astype(jnp.int32)
        slot = jnp.searchsorted(distinct, flat_ids).astype(jnp.int32)
        weighted = (hard_weight.astype(jnp.float32)[:, :, None] * query_hat.astype(jnp.float32)[:, None, :]).reshape(-1, feature_dim)
        hard_part = (logit_scale * jax.ops.segment_sum(weighted, slot, num_segments=devices_all * CAP)).astype(jnp.bfloat16)
        accum = accum.at[distinct].add(hard_part.astype(jnp.float32), mode='drop')
        return (accum, (query_grads, losses))
    accum = jnp.zeros(passages.shape, jnp.float32)
    inputs = (jnp.arange(devices_all, dtype=jnp.int32), queries.reshape(devices_all, Q_DEV, feature_dim), positives.reshape(devices_all, Q_DEV), hard_ids.reshape(devices_all, Q_DEV, HARD))
    passage_sum, outputs = lax.scan(device_step, accum, inputs)
    query_grads, losses = outputs
    passage_grads = ((passage_sum - passage_unit * lax.optimization_barrier(jnp.sum(passage_unit * passage_sum, axis=1, keepdims=True))) / passage_norm).astype(jnp.bfloat16)
    return (query_grads.reshape(queries.shape), passage_grads, losses.reshape(-1))
```

```python
import jax
import jax.numpy as jnp
from jax import lax
from jax.experimental import pallas as pl
from jax.experimental.pallas import tpu as pltpu
from jax.sharding import PartitionSpec as P

D = 4096
Q = 512
PB = 64
HARD = 8
CAP = 4
SCALE = 20.0
EPS = 1e-06
CH = 256
SL = 128
PARTS = 2
PW = D // PARTS
TN = 512
FWD_STEPS = ((0, 0), (0, 1), (1, 0), (3, 0), (1, 1), (3, 1), (2, 0), (2, 1))
BWD_STEPS = ((2, 0), (2, 1), (1, 0), (3, 0), (1, 1), (3, 1), (0, 0), (0, 1))
MESH = pl.DeviceIdType.MESH
F32 = jnp.float32
BF16 = jnp.bfloat16
NT = (((1,), (1,)), ((), ()))
TN_DIMS = (((0,), (0,)), ((), ()))


def iota(shape, dim):
    return lax.broadcasted_iota(jnp.int32, shape, dim)


def inv_rel(rel):
    return ((4 - rel // 2) % 4) * 2 + rel % 2


def dot(a, b):
    return jnp.dot(a, b, preferred_element_type=F32)


def onehot(mask):
    return jnp.where(mask, 1.0, 0.0).astype(BF16)


def kernel(
    passages, queries, ids_ref, out_q, out_p, out_l,
    pv, qv, qhat, hat, fsend, fetched, sret, part, sibr, z2m, z2p, z1m, z1p, xr,
    exp_c, exp_h, wc, wct, wh, wht, qsum, sel, selt, tabs, qinv, key_ref, kk_ref,
    lsem, ag_s, ag_r, tab_s, tab_r, f_s, f_r, r_s, r_r, rs_s, rs_r,
):
    blk = lax.axis_index("blk")
    grp = lax.axis_index("group")
    xh, z, core = blk // 8, (blk // 2) % 4, blk % 2
    y, xl = grp // 2, grp % 2

    def dev(dxh=0, dz=0, dc=0, dy=0, dxl=0):
        return (
            ((xh + dxh) % 2) * 8 + ((z + dz) % 4) * 2 + (core + dc) % 2,
            ((y + dy) % 4) * 2 + (xl + dxl) % 2,
        )

    sib, zp, zm, xo = dev(dc=1), dev(dz=1), dev(dz=3), dev(dxh=1)
    partner = [
        dev(dy=rel // 2, dxl=rel % 2, dxh=(rel % 2) & (rel // 2 % 2)) for rel in range(8)
    ]

    barrier = pltpu.get_barrier_semaphore()
    for d in [sib, zp, zm, xo] + partner[1:]:
        pl.semaphore_signal(barrier, inc=1, device_id=d, device_id_type=MESH)

    load_p = pltpu.make_async_copy(passages, pv, lsem.at[0])
    load_q = pltpu.make_async_copy(queries, qv, lsem.at[1])
    load_p.start()
    load_q.start()

    def remote(src, dst, ss, rs, d):
        return pltpu.make_async_remote_copy(
            src_ref=src, dst_ref=dst, send_sem=ss, recv_sem=rs, device_id=d, device_id_type=MESH
        )

    def cols(part_id):
        return pl.ds(part_id * PW, PW)

    ag = {}

    def row(dz, dc, dxh):
        return dz * CH + dc * 2 * PB + dxh * PB

    def add_ag(name, src, dst, d, parts=(0, 1)):
        for cq in parts:
            i = len(ag)
            ag[name, cq] = remote(
                hat.at[pl.ds(src, PB), cols(cq)], hat.at[pl.ds(dst, PB), cols(cq)],
                ag_s.at[i], ag_r.at[i], d,
            )

    own = row(0, 0, 0)
    add_ag("x", own, row(0, 0, 1), xo)
    add_ag("m0", own, row(3, 0, 0), zp)
    add_ag("p0", own, row(1, 0, 0), zm)
    add_ag("s00", own, row(0, 1, 0), sib)
    add_ag("s01", row(0, 0, 1), row(0, 1, 1), sib)
    add_ag("m1", row(0, 0, 1), row(3, 0, 1), zp)
    add_ag("p1", row(0, 0, 1), row(1, 0, 1), zm)
    for dxh in range(2):
        add_ag(f"s3{dxh}", row(3, 0, dxh), row(3, 1, dxh), sib)
        add_ag(f"s1{dxh}", row(1, 0, dxh), row(1, 1, dxh), sib)
        add_ag(f"t{dxh}", row(3, 0, dxh), row(2, 0, dxh), zp, (0,))
        add_ag(f"t{dxh}", row(1, 0, dxh), row(2, 0, dxh), zm, (1,))
        add_ag(f"s2{dxh}", row(2, 0, dxh), row(2, 1, dxh), sib)

    fetch, back = {}, {}
    for step, (j, cq) in enumerate(FWD_STEPS):
        for rel in range(1, 8):
            to = inv_rel(rel)
            fetch[j, cq, rel] = remote(
                fsend.at[pl.ds(j * SL + rel * 16, 16), cols(cq)],
                fetched.at[pl.ds(j * SL + to * 16, 16), cols(cq)],
                f_s.at[step, rel], f_r.at[step, to], partner[rel],
            )
    for step, (j, cq) in enumerate(BWD_STEPS):
        for rel in range(1, 8):
            to = inv_rel(rel)
            back[j, cq, rel] = remote(
                fsend.at[pl.ds(j * SL + rel * 16, 16), cols(cq)],
                sret.at[pl.ds(j * SL + to * 16, 16), cols(cq)],
                r_s.at[step, rel], r_r.at[step, to], partner[rel],
            )

    rs = {}

    def add_rs(name, src, dst, d):
        i = len(rs)
        rs[name] = remote(src, dst, rs_s.at[i], rs_r.at[i], d)

    for j, cq in BWD_STEPS:
        add_rs(
            ("sib", j, cq),
            part.at[pl.ds(j * CH + SL, SL), cols(cq)], sibr.at[pl.ds(j * SL, SL), cols(cq)], sib,
        )
    add_rs(("z", 2, 0), part.at[pl.ds(2 * CH, SL), cols(0)], z2m, zp)
    add_rs(("z", 2, 1), part.at[pl.ds(2 * CH, SL), cols(1)], z2p, zm)
    for cq in range(PARTS):
        add_rs(("z", 1, cq), part.at[pl.ds(CH, SL), cols(cq)], z1m.at[:, cols(cq)], zp)
        add_rs(("z", 3, cq), part.at[pl.ds(3 * CH, SL), cols(cq)], z1p.at[:, cols(cq)], zm)
        add_rs(("x", cq), part.at[pl.ds(PB, PB), cols(cq)], xr.at[:, cols(cq)], xo)

    load_p.wait()
    raw = pv[...].astype(F32)
    pinv = 1.0 / jnp.sqrt(jnp.sum(raw * raw, axis=1, keepdims=True) + EPS)
    hat[pl.ds(own, PB), :] = (raw * pinv).astype(BF16)
    pl.semaphore_wait(barrier, 11)
    for cq in range(PARTS):
        for name in ("x", "m0", "p0", "s00"):
            ag[name, cq].start()

    ids = ids_ref[...]
    owner = lax.shift_right_logical(ids, 6)
    ob, og = lax.shift_right_logical(owner, 3), owner & 7
    rel_g = ((lax.shift_right_logical(og, 1) - y) & 3) * 2 + ((og & 1) ^ xl)
    rel_b = (
        ((lax.shift_right_logical(ob, 1) - z) & 3) * 4
        + ((ob & 1) ^ core) * 2
        + (lax.shift_right_logical(ob, 3) ^ xh)
    )
    keys = (rel_g * 16 + rel_b) * 64 + (ids & 63)
    key_ref[...] = keys
    count = jnp.zeros((128, 128), F32)
    lane_q = iota((Q, 128), 1)
    for h in range(HARD):
        column = keys[:, h : h + 1]
        hi = onehot(lax.shift_right_logical(column, 6) == lane_q)
        lo = onehot((column & 63) == lane_q)
        count = count + lax.dot_general(lo, hi, TN_DIMS, preferred_element_type=F32)
    present = count > 0.5
    sub = iota((128, 128), 0)
    rank = dot(onehot(iota((128, 128), 1) < sub), onehot(present))
    table = jnp.zeros((8, 128), F32)
    for slot in range(CAP):
        hit = jnp.where(
            jnp.logical_and(present, rank == float(slot)), (sub + 1).astype(F32), 0.0
        )
        found = jnp.sum(hit, axis=0, keepdims=True) - 1.0
        table = jnp.where(iota((8, 128), 0) == slot, found, table)
    tabs[0] = table
    ask = []
    for rel in range(1, 8):
        to = inv_rel(rel)
        ask.append(remote(tabs.at[0], tabs.at[to], tab_s.at[rel], tab_r.at[to], partner[rel]))
        ask[-1].start()

    load_q.wait()

    def norm_rows(i, carry):
        rows = pl.ds(pl.multiple_of(i * 32, 32), 32)
        values = qv[rows, :].astype(F32)
        inverse = 1.0 / jnp.sqrt(jnp.sum(values * values, axis=1, keepdims=True) + EPS)
        qinv[rows, :] = jnp.broadcast_to(inverse, (32, 128))
        qhat[rows, :] = (values * inverse).astype(BF16)
        return carry

    def norm_queries(first, last):
        lax.fori_loop(first, last, norm_rows, 0)

    def build_selection():
        everything = tabs[...].reshape(64, 128).astype(BF16)
        lane = iota((128, 128), 1)
        who, o, slot = lane >> 4, (lane >> 2) & 3, lane & 3
        back_rel = ((4 - (who >> 1)) & 3) * 2 + (who & 1)
        flip = (who & 1) & ((who >> 1) & 1)
        offset = (o >> 1) * 128 + ((o & 1) ^ flip) * 64
        diag = iota((64, 128), 0) == (who * 8 + slot)[:64]
        for j in range(4):
            pick = onehot(iota((128, 128), 0) == back_rel * 16 + j * 4 + o)
            local = jnp.sum(jnp.where(diag, dot(everything, pick), 0.0), axis=0, keepdims=True)
            target = jnp.where(local >= 0.0, local + offset[:1].astype(F32), -1.0)
            match = jnp.where(iota((CH, SL), 0).astype(F32) == target, 1.0, 0.0)
            selt[pl.ds(j * CH, CH), :] = match.astype(BF16)
            sel[pl.ds(j * SL, SL), :] = jnp.transpose(match).astype(BF16)

    def build_mask():
        lane = iota((128, Q), 1)
        from_lane = ((lane >> 4) & 7) * 16 + (lane >> 7) * 4 + ((lane >> 2) & 3)
        spread = dot(table.astype(BF16), onehot(iota((128, Q), 0) == from_lane))
        local = jnp.sum(
            jnp.where(iota((8, Q), 0) == (lane & 3)[:8], spread, 0.0), axis=0, keepdims=True
        )
        wanted = jnp.where(local >= 0.0, from_lane[:1] * 64 + local.astype(jnp.int32), -1)

        def rows_mask(i, carry):
            rows = pl.ds(pl.multiple_of(i * 64, 64), 64)
            mine = key_ref[rows, :]
            found = mine[:, 0:1] == wanted
            for h in range(1, HARD):
                found = jnp.logical_or(found, mine[:, h : h + 1] == wanted)
            exp_h[rows, :] = jnp.where(found, 1.0, 0.0)
            return carry

        lax.fori_loop(0, Q // 64, rows_mask, 0)

    def select(j, cq):
        def tile(n, carry):
            at = pl.ds(pl.multiple_of(cq * PW + n * TN, TN), TN)
            rows = dot(sel[pl.ds(j * SL, SL), :], hat[pl.ds(j * CH, CH), at]).astype(BF16)
            fsend[pl.ds(j * SL, SL), at] = rows
            fetched[pl.ds(j * SL, 16), at] = rows[:16]
            return carry

        lax.fori_loop(0, PW // TN, tile, 0)
        for rel in range(1, 8):
            fetch[j, cq, rel].start()

    totals = {"cycle": jnp.zeros((Q, 1), F32), "pos": jnp.zeros((Q, 1), F32)}

    def cycle_scores(j):
        scores = SCALE * lax.dot_general(
            qhat[...], hat[pl.ds(j * CH, CH), :], NT, preferred_element_type=F32
        )
        raised = jnp.exp(scores)
        exp_c[:, pl.ds(j * CH, CH)] = raised
        positive = kk_ref[...] == iota((Q, CH), 1) + j * CH
        totals["cycle"] = totals["cycle"] + jnp.sum(raised, axis=1, keepdims=True)
        totals["pos"] = totals["pos"] + jnp.sum(
            jnp.where(positive, scores, 0.0), axis=1, keepdims=True
        )

    positives = ids[:, HARD : HARD + 1]
    pb = lax.shift_right_logical(positives, 6)
    kk_ref[...] = (
        ((lax.shift_right_logical(pb, 1) - z) & 3) * CH
        + ((pb & 1) ^ core) * 128
        + (lax.shift_right_logical(pb, 3) ^ xh) * 64
        + (positives & 63)
    )

    def relay_x(cq):
        ag["x", cq].wait_recv()
        for name in ("s01", "m1", "p1"):
            ag[name, cq].start()

    def relay_z(dxh, cq):
        ag[f"m{dxh}", cq].wait_recv()
        ag[f"s3{dxh}", cq].start()
        if cq == 0:
            ag[f"t{dxh}", 0].start()
        ag[f"p{dxh}", cq].wait_recv()
        ag[f"s1{dxh}", cq].start()
        if cq == 1:
            ag[f"t{dxh}", 1].start()

    def relay_two(dxh, cq):
        ag[f"t{dxh}", cq].wait_recv()
        ag[f"s2{dxh}", cq].start()

    def from_sib(j, cq):
        for dxh in range(2):
            ag[f"s{j}{dxh}", cq].wait_recv()

    for copy in ask:
        copy.wait_recv()
    build_selection()
    norm_queries(0, 6)
    relay_x(0)
    relay_z(0, 0)
    from_sib(0, 0)
    select(0, 0)
    norm_queries(6, 16)
    relay_x(1)
    relay_z(0, 1)
    from_sib(0, 1)
    select(0, 1)
    cycle_scores(0)
    relay_z(1, 0)
    from_sib(1, 0)
    select(1, 0)
    from_sib(3, 0)
    select(3, 0)
    relay_two(0, 0)
    relay_two(0, 1)
    relay_z(1, 1)
    from_sib(1, 1)
    select(1, 1)
    from_sib(3, 1)
    select(3, 1)
    cycle_scores(1)
    relay_two(1, 0)
    relay_two(1, 1)
    from_sib(2, 0)
    select(2, 0)
    from_sib(2, 1)
    select(2, 1)
    cycle_scores(3)
    cycle_scores(2)
    build_mask()

    pos_score = totals["pos"]
    pos_exp = jnp.exp(pos_score)
    hard_total = pos_exp
    for j in (0, 1, 3, 2):
        for cq in range(PARTS):
            for rel in range(1, 8):
                fetch[j, cq, rel].wait_recv()
        at = pl.ds(j * SL, SL)
        scores = SCALE * lax.dot_general(
            qhat[...], fetched[at, :], NT, preferred_element_type=F32
        )
        raised = exp_h[:, at] * jnp.exp(scores)
        exp_h[:, at] = raised
        hard_total = hard_total + jnp.sum(raised, axis=1, keepdims=True)
    for copy in fetch.values():
        copy.wait_send()
    hard_inv = 1.0 / hard_total

    def back_step(j, cq):
        def tile(n, carry):
            at = pl.ds(pl.multiple_of(cq * PW + n * TN, TN), TN)
            rows = (SCALE * dot(wht[pl.ds(j * SL, SL), :], qhat[:, at])).astype(BF16)
            fsend[pl.ds(j * SL, SL), at] = rows
            sret[pl.ds(j * SL, 16), at] = rows[:16]
            return carry

        lax.fori_loop(0, PW // TN, tile, 0)
        for rel in range(1, 8):
            back[j, cq, rel].start()

    for j in (2, 1, 3, 0):
        weights = exp_h[:, pl.ds(j * SL, SL)] * hard_inv
        wh[:, pl.ds(j * SL, SL)] = weights.astype(BF16)
        wht[pl.ds(j * SL, SL), :] = jnp.transpose(weights).astype(BF16)
    for j, cq in BWD_STEPS:
        back_step(j, cq)

    cycle_total = totals["cycle"]
    out_l[...] = jnp.log(cycle_total) + jnp.log(hard_total) - 2.0 * pos_score
    cycle_inv = 1.0 / cycle_total
    correction = 2.0 - pos_exp * hard_inv
    for j in (2, 1, 3, 0):
        at = pl.ds(j * CH, CH)
        positive = kk_ref[...] == iota((Q, CH), 1) + j * CH
        weights = exp_c[:, at] * cycle_inv - jnp.where(positive, correction, 0.0)
        wc[:, at] = weights.astype(BF16)
        wct[at, :] = jnp.transpose(weights).astype(BF16)

    QR = 128
    store_q = []

    def query_rows(block):
        rows = pl.ds(block * QR, QR)
        inverse = qinv[rows, 0:1]

        def product(n, total):
            at = pl.ds(pl.multiple_of(n * TN, TN), TN)
            tile = SCALE * (dot(wc[rows, :], hat[:, at]) + dot(wh[rows, :], fetched[:, at]))
            qsum[:, at] = tile
            unit = qv[rows, at].astype(F32) * inverse
            return total + jnp.sum(unit * tile, axis=1, keepdims=True)

        along = lax.fori_loop(0, D // TN, product, jnp.zeros((QR, 1), F32))

        def project(n, carry):
            at = pl.ds(pl.multiple_of(n * TN, TN), TN)
            unit = qv[rows, at].astype(F32) * inverse
            qv[rows, at] = ((qsum[:, at] - unit * along) * inverse).astype(BF16)
            return carry

        lax.fori_loop(0, D // TN, project, 0)
        store_q.append(
            pltpu.make_async_copy(qv.at[rows, :], out_q.at[rows, :], lsem.at[2 + block])
        )
        store_q[-1].start()

    def partial(j, cq):
        for rel in range(1, 8):
            back[j, cq, rel].wait_recv()

        def tile(n, carry):
            at = pl.ds(pl.multiple_of(cq * PW + n * TN, TN), TN)
            total = SCALE * dot(wct[pl.ds(j * CH, CH), :], qhat[:, at]) + dot(
                selt[pl.ds(j * CH, CH), :], sret[pl.ds(j * SL, SL), at]
            )
            part[pl.ds(j * CH, CH), at] = total.astype(BF16)
            return carry

        lax.fori_loop(0, PW // TN, tile, 0)
        rs["sib", j, cq].start()

    def reduce(j, cq):
        at = cols(cq)
        mine = pl.ds(j * CH, SL)
        rs["sib", j, cq].wait_recv()
        total = part[mine, at].astype(F32) + sibr[pl.ds(j * SL, SL), at].astype(F32)
        if (j, cq) == (1, 0):
            rs["z", 2, 0].wait_recv()
            total = total + z2m[...].astype(F32)
        if (j, cq) == (3, 1):
            rs["z", 2, 1].wait_recv()
            total = total + z2p[...].astype(F32)
        if j == 0:
            rs["z", 1, cq].wait_recv()
            rs["z", 3, cq].wait_recv()
            total = total + z1m[:, at].astype(F32) + z1p[:, at].astype(F32)
        part[mine, at] = total.astype(BF16)
        if j == 0:
            rs["x", cq].start()
        else:
            rs["z", j, cq].start()

    query_rows(0)
    partial(2, 0)
    partial(2, 1)
    reduce(2, 0)
    reduce(2, 1)
    query_rows(1)
    partial(1, 0)
    partial(3, 0)
    reduce(1, 0)
    reduce(3, 0)
    query_rows(2)
    partial(1, 1)
    partial(3, 1)
    reduce(1, 1)
    reduce(3, 1)
    query_rows(3)
    partial(0, 0)
    partial(0, 1)
    reduce(0, 0)
    reduce(0, 1)

    unit = pv[...].astype(F32) * pinv
    for cq in range(PARTS):
        rs["x", cq].wait_recv()
    total = part[pl.ds(0, PB), :].astype(F32) + xr[...].astype(F32)
    along = jnp.sum(unit * total, axis=1, keepdims=True)
    out_p[...] = ((total - unit * along) * pinv).astype(BF16)

    for copy in ask + list(ag.values()) + list(back.values()) + list(rs.values()):
        copy.wait_send()
    for copy in store_q:
        copy.wait()


def shards(queries, passages, positives, hard_ids):
    ids = jnp.concatenate([hard_ids, positives[:, None]], axis=1)
    dma = pltpu.SemaphoreType.DMA
    any_spec = pl.BlockSpec(memory_space=pl.ANY)
    vmem_spec = pl.BlockSpec(memory_space=pltpu.VMEM)
    query_grads, passage_grads, losses = pl.pallas_call(
        kernel,
        out_shape=(
            jax.ShapeDtypeStruct((Q, D), BF16),
            jax.ShapeDtypeStruct((PB, D), BF16),
            jax.ShapeDtypeStruct((Q, 1), F32),
        ),
        in_specs=[any_spec, any_spec, vmem_spec],
        out_specs=(any_spec, vmem_spec, vmem_spec),
        scratch_shapes=[
            pltpu.VMEM((PB, D), BF16),
            pltpu.VMEM((Q, D), BF16),
            pltpu.VMEM((Q, D), BF16),
            pltpu.VMEM((4 * CH, D), BF16),
            pltpu.VMEM((4 * SL, D), BF16),
            pltpu.VMEM((4 * SL, D), BF16),
            pltpu.VMEM((4 * SL, D), BF16),
            pltpu.VMEM((4 * CH, D), BF16),
            pltpu.VMEM((4 * SL, D), BF16),
            pltpu.VMEM((SL, PW), BF16),
            pltpu.VMEM((SL, PW), BF16),
            pltpu.VMEM((SL, D), BF16),
            pltpu.VMEM((SL, D), BF16),
            pltpu.VMEM((PB, D), BF16),
            pltpu.VMEM((Q, 4 * CH), F32),
            pltpu.VMEM((Q, 4 * SL), F32),
            pltpu.VMEM((Q, 4 * CH), BF16),
            pltpu.VMEM((4 * CH, Q), BF16),
            pltpu.VMEM((Q, 4 * SL), BF16),
            pltpu.VMEM((4 * SL, Q), BF16),
            pltpu.VMEM((128, D), F32),
            pltpu.VMEM((4 * SL, CH), BF16),
            pltpu.VMEM((4 * CH, SL), BF16),
            pltpu.VMEM((8, 8, 128), F32),
            pltpu.VMEM((Q, 128), F32),
            pltpu.VMEM((Q, HARD + 1), jnp.int32),
            pltpu.VMEM((Q, 1), jnp.int32),
            dma((8,)),
            dma((32,)), dma((32,)),
            dma((8,)), dma((8,)),
            dma((8, 8)), dma((8, 8)),
            dma((8, 8)), dma((8, 8)),
            dma((16,)), dma((16,)),
        ],
        compiler_params=pltpu.CompilerParams(
            collective_id=0, has_side_effects=True, vmem_limit_bytes=63 * 2**20
        ),
        cost_estimate=pl.CostEstimate(
            flops=6 * Q * 1536 * D, bytes_accessed=4 * Q * D, transcendentals=Q * 1536
        ),
    )(passages, queries, ids)
    return query_grads, passage_grads, losses.reshape(Q)


def solution(mesh):
    in_specs = (
        P(("blk", "group"), None),
        P(("blk", "group"), None),
        P(("blk", "group")),
        P(("blk", "group"), None),
    )
    out_specs = (P(("blk", "group"), None), P(("blk", "group"), None), P(("blk", "group")))
    return jax.shard_map(shards, mesh=mesh, in_specs=in_specs, out_specs=out_specs, check_vma=False)
```

```python
import jax
import jax.numpy as jnp
from jax import lax
from jax.experimental import pallas as pl
from jax.experimental.pallas import tpu as pltpu
from jax.sharding import PartitionSpec as P

D = 4096
Q = 512
PB = 64
HARD = 8
CAP = 4
SCALE = 20.0
EPS = 1e-06
CH = 256
SL = 128
PARTS = 4
PW = D // PARTS
TN = 512
HALF = PARTS // 2
ALL_PARTS = tuple(range(PARTS))
DEPTH = 3
STEPS = 4 * PARTS
BWD_STEPS = tuple((j, cq) for j in (3, 2, 1, 0) for cq in ALL_PARTS)
MESH = pl.DeviceIdType.MESH
F32 = jnp.float32
BF16 = jnp.bfloat16
NT = (((1,), (1,)), ((), ()))
TN_DIMS = (((0,), (0,)), ((), ()))


def iota(shape, dim):
    return lax.broadcasted_iota(jnp.int32, shape, dim)


def inv_rel(rel):
    return ((4 - rel // 2) % 4) * 2 + rel % 2


def flips(rel):
    return (rel % 2) & (rel // 2 % 2)


def seen_by(rel, j):
    return (0, 2, 1, 3)[j] if flips(rel) else j


def dot(a, b):
    return jnp.dot(a, b, preferred_element_type=F32)


def onehot(mask):
    return jnp.where(mask, 1.0, 0.0).astype(BF16)


def kernel(
    passages, queries, ids_ref, out_q, out_p, out_l,
    pv, qv, qhat, hat, fsend, fetched, sret, part, sibr, z2, z1m, z1p, xr,
    exp_c, exp_h, wc, wct, wh, wht, qsum, sel, selt, tabs, qinv, key_ref, kk_ref,
    lsem, ag_s, ag_r, tab_s, tab_r, f_s, f_r, r_s, r_r, rs_s, rs_r,
):
    blk = lax.axis_index("blk")
    grp = lax.axis_index("group")
    xh, z, core = blk // 8, (blk // 2) % 4, blk % 2
    y, xl = grp // 2, grp % 2

    def dev(dxh=0, dz=0, dc=0, dy=0, dxl=0):
        return (
            ((xh + dxh) % 2) * 8 + ((z + dz) % 4) * 2 + (core + dc) % 2,
            ((y + dy) % 4) * 2 + (xl + dxl) % 2,
        )

    sib, zp, zm, xo = dev(dc=1), dev(dz=1), dev(dz=3), dev(dxh=1)
    partner = [
        dev(dy=rel // 2, dxl=rel % 2, dxh=flips(rel)) for rel in range(8)
    ]

    barrier = pltpu.get_barrier_semaphore()
    for d in [sib, zp, zm, xo] + partner[1:]:
        pl.semaphore_signal(barrier, inc=1, device_id=d, device_id_type=MESH)

    load_p = pltpu.make_async_copy(passages, pv, lsem.at[0])
    load_q = pltpu.make_async_copy(queries, qv, lsem.at[1])
    load_p.start()
    load_q.start()

    def remote(src, dst, ss, rs, d):
        return pltpu.make_async_remote_copy(
            src_ref=src, dst_ref=dst, send_sem=ss, recv_sem=rs, device_id=d, device_id_type=MESH
        )

    def cols(part_id):
        return pl.ds(part_id * PW, PW)

    ag = {}

    def row(dz, dc, dxh):
        chunk, side = (1 + dxh, dz // 2) if dz % 2 else (dz // 2 * 3, dxh)
        return chunk * CH + dc * 2 * PB + side * PB

    def add_ag(name, src, dst, d, parts=ALL_PARTS):
        for cq in parts:
            i = len(ag)
            ag[name, cq] = remote(
                hat.at[pl.ds(src, PB), cols(cq)], hat.at[pl.ds(dst, PB), cols(cq)],
                ag_s.at[i], ag_r.at[i], d,
            )

    own = row(0, 0, 0)
    add_ag("x", own, row(0, 0, 1), xo)
    add_ag("m0", own, row(3, 0, 0), zp)
    add_ag("p0", own, row(1, 0, 0), zm)
    add_ag("s00", own, row(0, 1, 0), sib)
    add_ag("s01", row(0, 0, 1), row(0, 1, 1), sib)
    add_ag("m1", row(0, 0, 1), row(3, 0, 1), zp)
    add_ag("p1", row(0, 0, 1), row(1, 0, 1), zm)
    for dxh in range(2):
        add_ag(f"s3{dxh}", row(3, 0, dxh), row(3, 1, dxh), sib)
        add_ag(f"s1{dxh}", row(1, 0, dxh), row(1, 1, dxh), sib)
        add_ag(f"t{dxh}", row(3, 0, dxh), row(2, 0, dxh), zp, ALL_PARTS[:HALF])
        add_ag(f"t{dxh}", row(1, 0, dxh), row(2, 0, dxh), zm, ALL_PARTS[HALF:])
        add_ag(f"s2{dxh}", row(2, 0, dxh), row(2, 1, dxh), sib)

    fetch, back = {}, {}
    for step, (j, cq) in enumerate(BWD_STEPS):
        for rel in range(1, 8):
            to, theirs = inv_rel(rel), seen_by(rel, j)
            fetch[j, cq, rel] = remote(
                fsend.at[pl.ds(j * SL + rel * 16, 16), cols(cq)],
                fetched.at[pl.ds(theirs * SL + to * 16, 16), cols(cq)],
                f_s.at[step, rel], f_r.at[step, to], partner[rel],
            )
            back[j, cq, rel] = remote(
                fsend.at[pl.ds(theirs * SL + rel * 16, 16), cols(cq)],
                sret.at[pl.ds(j * SL + to * 16, 16), cols(cq)],
                r_s.at[step, rel], r_r.at[step, to], partner[rel],
            )

    rs = {}

    def add_rs(name, src, dst, d):
        i = len(rs)
        rs[name] = remote(src, dst, rs_s.at[i], rs_r.at[i], d)

    for j, cq in BWD_STEPS:
        add_rs(
            ("sib", j, cq),
            part.at[pl.ds(j * CH + SL, SL), cols(cq)], sibr.at[pl.ds(j * SL, SL), cols(cq)], sib,
        )
    for cq in ALL_PARTS:
        add_rs(
            ("z", 3, cq),
            part.at[pl.ds(3 * CH, SL), cols(cq)], z2.at[:, cols(cq)], zp if cq < HALF else zm,
        )
        for j in (2, 1):
            there = pl.ds((j - 1) * PB, PB)
            add_rs(
                ("zp", j, cq), part.at[pl.ds(j * CH, PB), cols(cq)], z1m.at[there, cols(cq)], zp
            )
            add_rs(
                ("zm", j, cq), part.at[pl.ds(j * CH + PB, PB), cols(cq)], z1p.at[there, cols(cq)], zm
            )
        add_rs(("x", cq), part.at[pl.ds(PB, PB), cols(cq)], xr.at[:, cols(cq)], xo)

    load_p.wait()
    raw = pv[...].astype(F32)
    pinv = 1.0 / jnp.sqrt(jnp.sum(raw * raw, axis=1, keepdims=True) + EPS)
    hat[pl.ds(own, PB), :] = (raw * pinv).astype(BF16)
    pl.semaphore_wait(barrier, 11)

    def own_send(cq):
        for name in ("x", "m0", "p0", "s00"):
            if cq >= 2:
                ag[name, cq - 2].wait_send()
                gone.add((name, cq - 2))
            ag[name, cq].start()

    gone = set()
    own_send(0)

    ids = ids_ref[...]
    owner = lax.shift_right_logical(ids, 6)
    ob, og = lax.shift_right_logical(owner, 3), owner & 7
    rel_g = ((lax.shift_right_logical(og, 1) - y) & 3) * 2 + ((og & 1) ^ xl)

    def place(block):
        dz = (lax.shift_right_logical(block, 1) - z) & 3
        dxh = lax.shift_right_logical(block, 3) ^ xh
        odd, far = (dz & 1) == 1, lax.shift_right_logical(dz, 1)
        chunk, side = jnp.where(odd, 1 + dxh, 3 * far), jnp.where(odd, far, dxh)
        return chunk, ((block & 1) ^ core) * 2 + side

    chunk, o = place(ob)
    rel_b = chunk * 4 + o
    keys = (rel_g * 16 + rel_b) * 64 + (ids & 63)
    key_ref[...] = keys
    count = jnp.zeros((128, 128), F32)
    lane_q = iota((Q, 128), 1)
    for h in range(HARD):
        column = keys[:, h : h + 1]
        hi = onehot(lax.shift_right_logical(column, 6) == lane_q)
        lo = onehot((column & 63) == lane_q)
        count = count + lax.dot_general(lo, hi, TN_DIMS, preferred_element_type=F32)
    present = count > 0.5
    sub = iota((128, 128), 0)
    rank = dot(onehot(iota((128, 128), 1) < sub), onehot(present))
    table = jnp.zeros((8, 128), F32)
    for slot in range(CAP):
        hit = jnp.where(
            jnp.logical_and(present, rank == float(slot)), (sub + 1).astype(F32), 0.0
        )
        found = jnp.sum(hit, axis=0, keepdims=True) - 1.0
        table = jnp.where(iota((8, 128), 0) == slot, found, table)
    tabs[0] = table
    ask = []
    for rel in range(1, 8):
        to = inv_rel(rel)
        ask.append(remote(tabs.at[0], tabs.at[to], tab_s.at[rel], tab_r.at[to], partner[rel]))
        ask[-1].start()

    load_q.wait()

    def norm_rows(i, carry):
        rows = pl.ds(pl.multiple_of(i * 32, 32), 32)
        values = qv[rows, :].astype(F32)
        inverse = 1.0 / jnp.sqrt(jnp.sum(values * values, axis=1, keepdims=True) + EPS)
        qinv[rows, :] = jnp.broadcast_to(inverse, (32, 128))
        qhat[rows, :] = (values * inverse).astype(BF16)
        return carry

    def norm_queries(first, last):
        lax.fori_loop(first, last, norm_rows, 0)

    def build_selection():
        everything = tabs[...].reshape(64, 128).astype(BF16)
        lane = iota((128, 128), 1)
        who, o, slot = lane >> 4, (lane >> 2) & 3, lane & 3
        back_rel = ((4 - (who >> 1)) & 3) * 2 + (who & 1)
        flip = (who & 1) & ((who >> 1) & 1)
        diag = iota((64, 128), 0) == (who * 8 + slot)[:64]
        for j in range(4):
            theirs = jnp.where(flip == 1, (0, 2, 1, 3)[j], j)
            offset = (o >> 1) * 128 + ((o & 1) ^ (flip if j in (0, 3) else 0)) * 64
            pick = onehot(iota((128, 128), 0) == back_rel * 16 + theirs * 4 + o)
            local = jnp.sum(jnp.where(diag, dot(everything, pick), 0.0), axis=0, keepdims=True)
            target = jnp.where(local >= 0.0, local + offset[:1].astype(F32), -1.0)
            match = jnp.where(iota((CH, SL), 0).astype(F32) == target, 1.0, 0.0)
            selt[pl.ds(j * CH, CH), :] = match.astype(BF16)
            sel[pl.ds(j * SL, SL), :] = jnp.transpose(match).astype(BF16)

    def build_mask():
        lane = iota((128, Q), 1)
        from_lane = ((lane >> 4) & 7) * 16 + (lane >> 7) * 4 + ((lane >> 2) & 3)
        spread = dot(table.astype(BF16), onehot(iota((128, Q), 0) == from_lane))
        local = jnp.sum(
            jnp.where(iota((8, Q), 0) == (lane & 3)[:8], spread, 0.0), axis=0, keepdims=True
        )
        wanted = jnp.where(local >= 0.0, from_lane[:1] * 64 + local.astype(jnp.int32), -1)

        def rows_mask(i, carry):
            rows = pl.ds(pl.multiple_of(i * 64, 64), 64)
            mine = key_ref[rows, :]
            found = mine[:, 0:1] == wanted
            for h in range(1, HARD):
                found = jnp.logical_or(found, mine[:, h : h + 1] == wanted)
            exp_h[rows, :] = jnp.where(found, 1.0, 0.0)
            return carry

        lax.fori_loop(0, Q // 64, rows_mask, 0)

    def select(j, cq):
        def tile(n, carry):
            at = pl.ds(pl.multiple_of(cq * PW + n * TN, TN), TN)
            rows = dot(sel[pl.ds(j * SL, SL), :], hat[pl.ds(j * CH, CH), at]).astype(BF16)
            fsend[pl.ds(j * SL, SL), at] = rows
            fetched[pl.ds(j * SL, 16), at] = rows[:16]
            return carry

        lax.fori_loop(0, PW // TN, tile, 0)
        for rel in range(1, 8):
            fetch[j, cq, rel].start()

    totals = {"cycle": jnp.zeros((Q, 1), F32), "pos": jnp.zeros((Q, 1), F32)}

    def cycle_scores(j):
        scores = SCALE * lax.dot_general(
            qhat[...], hat[pl.ds(j * CH, CH), :], NT, preferred_element_type=F32
        )
        raised = jnp.exp(scores)
        exp_c[:, pl.ds(j * CH, CH)] = raised
        positive = kk_ref[...] == iota((Q, CH), 1) + j * CH
        totals["cycle"] = totals["cycle"] + jnp.sum(raised, axis=1, keepdims=True)
        totals["pos"] = totals["pos"] + jnp.sum(
            jnp.where(positive, scores, 0.0), axis=1, keepdims=True
        )

    positives = ids[:, HARD : HARD + 1]
    pb = lax.shift_right_logical(positives, 6)
    chunk, o = place(pb)
    kk_ref[...] = chunk * CH + o * PB + (positives & 63)

    def sib_relay(cq, *names):
        for came, sent in names:
            ag[came, cq].wait_recv()
            ag[sent, cq].start()

    def z_relay(dxh, cq):
        ag[f"t{dxh}", cq].start()

    def from_sib(cq, *names):
        for name in names:
            ag[name, cq].wait_recv()

    own_send(1)
    norm_queries(0, 4)
    for copy in ask:
        copy.wait_recv()
    build_selection()
    for cq in ALL_PARTS:
        sib_relay(cq, ("x", "s01"), ("m0", "s30"), ("p0", "s10"))
        if cq + 2 < PARTS:
            own_send(cq + 2)
        if cq > 0:
            ag["m1", cq - 1].start()
            ag["p1", cq - 1].start()
        norm_queries(4 + 3 * cq, 7 + 3 * cq)
        from_sib(cq, "s00", "s01")
        select(0, cq)
        from_sib(cq, "s30", "s10")
        select(1, cq)
    ag["m1", PARTS - 1].start()
    ag["p1", PARTS - 1].start()
    for cq in ALL_PARTS:
        z_relay(0, cq)
    for cq in ALL_PARTS:
        sib_relay(cq, ("m1", "s31"), ("p1", "s11"))
        z_relay(1, cq)
        if cq < 2:
            cycle_scores(cq)
        from_sib(cq, "s31", "s11")
        select(2, cq)
    for cq in ALL_PARTS:
        sib_relay(cq, ("t0", "s20"), ("t1", "s21"))
        if cq == 0:
            cycle_scores(2)
        from_sib(cq, "s20", "s21")
        select(3, cq)
    cycle_scores(3)
    build_mask()

    pos_score = totals["pos"]
    pos_exp = jnp.exp(pos_score)
    hard_total = pos_exp
    for step in ((0, 1, 2), (3,)):
        for j in step:
            for cq in ALL_PARTS:
                for rel in range(1, 8):
                    fetch[j, cq, rel].wait_recv()
        at = pl.ds(step[0] * SL, len(step) * SL)
        scores = SCALE * lax.dot_general(
            qhat[...], fetched[at, :], NT, preferred_element_type=F32
        )
        raised = exp_h[:, at] * jnp.exp(scores)
        exp_h[:, at] = raised
        hard_total = hard_total + jnp.sum(raised, axis=1, keepdims=True)
    for copy in fetch.values():
        copy.wait_send()
    hard_inv = 1.0 / hard_total

    def back_sums(j):
        weights = exp_h[:, pl.ds(j * SL, SL)] * hard_inv
        wh[:, pl.ds(j * SL, SL)] = weights.astype(BF16)
        wht[pl.ds(j * SL, SL), :] = jnp.transpose(weights).astype(BF16)

        def tile(n, carry):
            at = pl.ds(pl.multiple_of(n * TN, TN), TN)
            rows = (SCALE * dot(wht[pl.ds(j * SL, SL), :], qhat[:, at])).astype(BF16)
            fsend[pl.ds(j * SL, SL), at] = rows
            sret[pl.ds(j * SL, 16), at] = rows[:16]
            return carry

        lax.fori_loop(0, D // TN, tile, 0)

    left = set()

    def back_start(step):
        j, cq = BWD_STEPS[step]
        for rel in range(1, 8):
            if step >= DEPTH:
                earlier = BWD_STEPS[step - DEPTH] + (rel,)
                back[earlier].wait_send()
                left.add(earlier)
            back[j, cq, rel].start()

    back_sums(3)
    for step in range(DEPTH):
        back_start(step)
    for j in (2, 1, 0):
        back_sums(j)

    cycle_total = totals["cycle"]
    losses = jnp.log(cycle_total) + jnp.log(hard_total) - 2.0 * pos_score
    for i in range(Q // 128):
        spread = jnp.broadcast_to(losses[i * 128 : (i + 1) * 128], (128, 128))
        out_l[pl.ds(i, 1), :] = jnp.transpose(spread)[:1]
    cycle_inv = 1.0 / cycle_total
    correction = 2.0 - pos_exp * hard_inv
    for j in (3, 2, 1, 0):
        at = pl.ds(j * CH, CH)
        positive = kk_ref[...] == iota((Q, CH), 1) + j * CH
        weights = exp_c[:, at] * cycle_inv - jnp.where(positive, correction, 0.0)
        wc[:, at] = weights.astype(BF16)
        wct[at, :] = jnp.transpose(weights).astype(BF16)

    QR = 128
    store_q = []

    def query_rows(block):
        rows = pl.ds(block * QR, QR)
        inverse = qinv[rows, 0:1]

        def product(n, total):
            at = pl.ds(pl.multiple_of(n * TN, TN), TN)
            tile = SCALE * (dot(wc[rows, :], hat[:, at]) + dot(wh[rows, :], fetched[:, at]))
            qsum[:, at] = tile
            unit = qv[rows, at].astype(F32) * inverse
            return total + jnp.sum(unit * tile, axis=1, keepdims=True)

        along = lax.fori_loop(0, D // TN, product, jnp.zeros((QR, 1), F32))

        def project(n, carry):
            at = pl.ds(pl.multiple_of(n * TN, TN), TN)
            unit = qv[rows, at].astype(F32) * inverse
            qv[rows, at] = ((qsum[:, at] - unit * along) * inverse).astype(BF16)
            return carry

        lax.fori_loop(0, D // TN, project, 0)
        store_q.append(
            pltpu.make_async_copy(qv.at[rows, :], out_q.at[rows, :], lsem.at[2 + block])
        )
        store_q[-1].start()

    def partial(j, cq):
        for rel in range(1, 8):
            back[j, cq, rel].wait_recv()

        def tile(n, carry):
            at = pl.ds(pl.multiple_of(cq * PW + n * TN, TN), TN)
            total = SCALE * dot(wct[pl.ds(j * CH, CH), :], qhat[:, at]) + dot(
                selt[pl.ds(j * CH, CH), :], sret[pl.ds(j * SL, SL), at]
            )
            part[pl.ds(j * CH, CH), at] = total.astype(BF16)
            return carry

        lax.fori_loop(0, PW // TN, tile, 0)
        rs["sib", j, cq].start()

    def reduce(j, cq):
        at = cols(cq)
        mine = pl.ds(j * CH, SL)
        rs["sib", j, cq].wait_recv()
        total = part[mine, at].astype(F32) + sibr[pl.ds(j * SL, SL), at].astype(F32)
        if j == 3:
            part[mine, at] = total.astype(BF16)
            rs["z", 3, cq].start()
        elif j > 0:
            here = pl.ds((j - 1) * PB, PB)
            rs["z", 3, cq].wait_recv() if j == 2 else None
            more = z2[here, at].astype(F32)
            first, second = total[:PB], total[PB:]
            if cq < HALF:
                first = first + more
            else:
                second = second + more
            part[pl.ds(j * CH, PB), at] = first.astype(BF16)
            rs["zp", j, cq].start()
            part[pl.ds(j * CH + PB, PB), at] = second.astype(BF16)
            rs["zm", j, cq].start()
        else:
            for dxh in (1, 0):
                rs["zp", 1 + dxh, cq].wait_recv()
                rs["zm", 1 + dxh, cq].wait_recv()
                here = pl.ds(dxh * PB, PB)
                both = z1m[here, at].astype(F32) + z1p[here, at].astype(F32)
                both = both + total[dxh * PB : (dxh + 1) * PB]
                if dxh == 1:
                    part[here, at] = both.astype(BF16)
                    rs["x", cq].start()
                else:
                    qsum[:PB, at] = both

    waiting = []
    for step, (j, cq) in enumerate(BWD_STEPS):
        partial(j, cq)
        if step + DEPTH < STEPS:
            back_start(step + DEPTH)
        waiting.append((j, cq))
        if len(waiting) > 1:
            reduce(*waiting.pop(0))
        if step % 2 == 1 and step // 2 < Q // QR:
            query_rows(step // 2)
    reduce(*waiting.pop(0))

    unit = pv[...].astype(F32) * pinv
    for cq in ALL_PARTS:
        rs["x", cq].wait_recv()
    total = qsum[:PB, :] + xr[...].astype(F32)
    along = jnp.sum(unit * total, axis=1, keepdims=True)
    out_p[...] = ((total - unit * along) * pinv).astype(BF16)

    for key, copy in ag.items():
        if key not in gone:
            copy.wait_send()
    for copy in ask + list(rs.values()):
        copy.wait_send()
    for key, copy in back.items():
        if key not in left:
            copy.wait_send()
    for copy in store_q:
        copy.wait()


def shards(queries, passages, positives, hard_ids):
    ids = jnp.concatenate([hard_ids, positives[:, None]], axis=1)
    dma = pltpu.SemaphoreType.DMA
    any_spec = pl.BlockSpec(memory_space=pl.ANY)
    vmem_spec = pl.BlockSpec(memory_space=pltpu.VMEM)
    query_grads, passage_grads, losses = pl.pallas_call(
        kernel,
        out_shape=(
            jax.ShapeDtypeStruct((Q, D), BF16),
            jax.ShapeDtypeStruct((PB, D), BF16),
            jax.ShapeDtypeStruct((Q // 128, 128), F32),
        ),
        in_specs=[any_spec, any_spec, vmem_spec],
        out_specs=(any_spec, vmem_spec, vmem_spec),
        scratch_shapes=[
            pltpu.VMEM((PB, D), BF16),
            pltpu.VMEM((Q, D), BF16),
            pltpu.VMEM((Q, D), BF16),
            pltpu.VMEM((4 * CH, D), BF16),
            pltpu.VMEM((4 * SL, D), BF16),
            pltpu.VMEM((4 * SL, D), BF16),
            pltpu.VMEM((4 * SL, D), BF16),
            pltpu.VMEM((4 * CH, D), BF16),
            pltpu.VMEM((4 * SL, D), BF16),
            pltpu.VMEM((SL, D), BF16),
            pltpu.VMEM((SL, D), BF16),
            pltpu.VMEM((SL, D), BF16),
            pltpu.VMEM((PB, D), BF16),
            pltpu.VMEM((Q, 4 * CH), F32),
            pltpu.VMEM((Q, 4 * SL), F32),
            pltpu.VMEM((Q, 4 * CH), BF16),
            pltpu.VMEM((4 * CH, Q), BF16),
            pltpu.VMEM((Q, 4 * SL), BF16),
            pltpu.VMEM((4 * SL, Q), BF16),
            pltpu.VMEM((128, D), F32),
            pltpu.VMEM((4 * SL, CH), BF16),
            pltpu.VMEM((4 * CH, SL), BF16),
            pltpu.VMEM((8, 8, 128), F32),
            pltpu.VMEM((Q, 128), F32),
            pltpu.VMEM((Q, HARD + 1), jnp.int32),
            pltpu.VMEM((Q, 1), jnp.int32),
            dma((8,)),
            dma((15 * PARTS,)), dma((15 * PARTS,)),
            dma((8,)), dma((8,)),
            dma((STEPS, 8)), dma((STEPS, 8)),
            dma((STEPS, 8)), dma((STEPS, 8)),
            dma((10 * PARTS,)), dma((10 * PARTS,)),
        ],
        compiler_params=pltpu.CompilerParams(
            collective_id=0, has_side_effects=True, vmem_limit_bytes=63 * 2**20
        ),
        cost_estimate=pl.CostEstimate(
            flops=6 * Q * 1536 * D, bytes_accessed=4 * Q * D, transcendentals=Q * 1536
        ),
    )(passages, queries, ids)
    return query_grads, passage_grads, losses.reshape(Q)


def solution(mesh):
    in_specs = (
        P(("blk", "group"), None),
        P(("blk", "group"), None),
        P(("blk", "group")),
        P(("blk", "group"), None),
    )
    out_specs = (P(("blk", "group"), None), P(("blk", "group"), None), P(("blk", "group")))
    return jax.shard_map(shards, mesh=mesh, in_specs=in_specs, out_specs=out_specs, check_vma=False)
```

```python
import jax
import jax.numpy as jnp
from jax import lax
from jax.experimental import pallas as pl
from jax.experimental.pallas import tpu as pltpu
from jax.sharding import PartitionSpec as P

D = 4096
Q = 512
PB = 64
HARD = 8
CAP = 4
SCALE = 20.0
EPS = 1e-06
CH = 256
SL = 128
PARTS = 4
PW = D // PARTS
TN = 512
HALF = PARTS // 2
ALL_PARTS = tuple(range(PARTS))
DEPTH = 6
STEPS = 4 * PARTS
BWD_STEPS = tuple((j, cq) for j in (3, 2, 1, 0) for cq in ALL_PARTS)
MESH = pl.DeviceIdType.MESH
F32 = jnp.float32
BF16 = jnp.bfloat16
NT = (((1,), (1,)), ((), ()))
TN_DIMS = (((0,), (0,)), ((), ()))


def iota(shape, dim):
    return lax.broadcasted_iota(jnp.int32, shape, dim)


def inv_rel(rel):
    return ((4 - rel // 2) % 4) * 2 + rel % 2


def flips(rel):
    return (rel % 2) & (rel // 2 % 2)


def seen_by(rel, j):
    return (0, 2, 1, 3)[j] if flips(rel) else j


def dot(a, b):
    return jnp.dot(a, b, preferred_element_type=F32)


def onehot(mask):
    return jnp.where(mask, 1.0, 0.0).astype(BF16)


def kernel(
    passages, queries, ids_ref, pos_ref, out_q, out_p, out_l,
    pv, qv, qhat, hat, fsend, fetched, sret, part, sibr, z2, z1m, z1p, xr,
    exp_c, exp_h, wc, wct, wh, wht, qsum, sel, selt, tabs, qinv, key_ref, kk_ref,
    lsem, ag_s, ag_r, tab_s, tab_r, f_s, f_r, r_s, r_r, rs_s, rs_r,
):
    blk = lax.axis_index("blk")
    grp = lax.axis_index("group")
    xh, z, core = blk // 8, (blk // 2) % 4, blk % 2
    y, xl = grp // 2, grp % 2

    def dev(dxh=0, dz=0, dc=0, dy=0, dxl=0):
        return (
            ((xh + dxh) % 2) * 8 + ((z + dz) % 4) * 2 + (core + dc) % 2,
            ((y + dy) % 4) * 2 + (xl + dxl) % 2,
        )

    sib, zp, zm, xo = dev(dc=1), dev(dz=1), dev(dz=3), dev(dxh=1)
    partner = [
        dev(dy=rel // 2, dxl=rel % 2, dxh=flips(rel)) for rel in range(8)
    ]

    barrier = pltpu.get_barrier_semaphore()
    for d in [sib, zp, zm, xo] + partner[1:]:
        pl.semaphore_signal(barrier, inc=1, device_id=d, device_id_type=MESH)

    load_p = pltpu.make_async_copy(passages, pv, lsem.at[0])
    load_q = pltpu.make_async_copy(queries, qv, lsem.at[1])
    load_p.start()
    load_q.start()

    def remote(src, dst, ss, rs, d):
        return pltpu.make_async_remote_copy(
            src_ref=src, dst_ref=dst, send_sem=ss, recv_sem=rs, device_id=d, device_id_type=MESH
        )

    def cols(part_id):
        return pl.ds(part_id * PW, PW)

    ag = {}

    def row(dz, dc, dxh):
        chunk, side = (1 + dxh, dz // 2) if dz % 2 else (dz // 2 * 3, dxh)
        return chunk * CH + dc * 2 * PB + side * PB

    def add_ag(name, src, dst, d, parts=ALL_PARTS):
        for cq in parts:
            i = len(ag)
            ag[name, cq] = remote(
                hat.at[pl.ds(src, PB), cols(cq)], hat.at[pl.ds(dst, PB), cols(cq)],
                ag_s.at[i], ag_r.at[i], d,
            )

    own = row(0, 0, 0)
    add_ag("x", own, row(0, 0, 1), xo)
    add_ag("m0", own, row(3, 0, 0), zp)
    add_ag("p0", own, row(1, 0, 0), zm)
    add_ag("s00", own, row(0, 1, 0), sib)
    add_ag("s01", row(0, 0, 1), row(0, 1, 1), sib)
    add_ag("m1", row(0, 0, 1), row(3, 0, 1), zp)
    add_ag("p1", row(0, 0, 1), row(1, 0, 1), zm)
    for dxh in range(2):
        add_ag(f"s3{dxh}", row(3, 0, dxh), row(3, 1, dxh), sib)
        add_ag(f"s1{dxh}", row(1, 0, dxh), row(1, 1, dxh), sib)
        add_ag(f"t{dxh}", row(3, 0, dxh), row(2, 0, dxh), zp, ALL_PARTS[:HALF])
        add_ag(f"t{dxh}", row(1, 0, dxh), row(2, 0, dxh), zm, ALL_PARTS[HALF:])
        add_ag(f"s2{dxh}", row(2, 0, dxh), row(2, 1, dxh), sib)

    fetch, back = {}, {}
    for step, (j, cq) in enumerate(BWD_STEPS):
        for rel in range(1, 8):
            to, theirs = inv_rel(rel), seen_by(rel, j)
            fetch[j, cq, rel] = remote(
                fsend.at[pl.ds(j * SL + rel * 16, 16), cols(cq)],
                fetched.at[pl.ds(theirs * SL + to * 16, 16), cols(cq)],
                f_s.at[step, rel], f_r.at[step, to], partner[rel],
            )
            back[j, cq, rel] = remote(
                fsend.at[pl.ds(theirs * SL + rel * 16, 16), cols(cq)],
                sret.at[pl.ds(j * SL + to * 16, 16), cols(cq)],
                r_s.at[step, rel], r_r.at[step, to], partner[rel],
            )

    rs = {}

    def add_rs(name, src, dst, d):
        i = len(rs)
        rs[name] = remote(src, dst, rs_s.at[i], rs_r.at[i], d)

    for j, cq in BWD_STEPS:
        add_rs(
            ("sib", j, cq),
            part.at[pl.ds(j * CH + SL, SL), cols(cq)], sibr.at[pl.ds(j * SL, SL), cols(cq)], sib,
        )
    for cq in ALL_PARTS:
        add_rs(
            ("z", 3, cq),
            part.at[pl.ds(3 * CH, SL), cols(cq)], z2.at[:, cols(cq)], zp if cq < HALF else zm,
        )
        for j in (2, 1):
            there = pl.ds((j - 1) * PB, PB)
            add_rs(
                ("zp", j, cq), part.at[pl.ds(j * CH, PB), cols(cq)], z1m.at[there, cols(cq)], zp
            )
            add_rs(
                ("zm", j, cq), part.at[pl.ds(j * CH + PB, PB), cols(cq)], z1p.at[there, cols(cq)], zm
            )
        add_rs(("x", cq), part.at[pl.ds(PB, PB), cols(cq)], xr.at[:, cols(cq)], xo)

    def place(block):
        dz = (lax.shift_right_logical(block, 1) - z) & 3
        dxh = lax.shift_right_logical(block, 3) ^ xh
        odd, far = (dz & 1) == 1, lax.shift_right_logical(dz, 1)
        chunk, side = jnp.where(odd, 1 + dxh, 3 * far), jnp.where(odd, far, dxh)
        return chunk, ((block & 1) ^ core) * 2 + side

    ids = ids_ref[...]
    owner = lax.shift_right_logical(ids, 6)
    og = owner & 7
    rel_g = ((lax.shift_right_logical(og, 1) - y) & 3) * 2 + ((og & 1) ^ xl)
    chunk, o = place(lax.shift_right_logical(owner, 3))
    keys = (rel_g * 16 + chunk * 4 + o) * 64 + (ids & 63)
    count = jnp.zeros((128, 128), F32)
    sub_q = iota((128, Q), 0)
    for h in range(HARD):
        key = keys[h : h + 1]
        hi = onehot(lax.shift_right_logical(key, 6) == sub_q)
        lo = onehot((key & 63) == sub_q)
        count = count + lax.dot_general(lo, hi, NT, preferred_element_type=F32)
    present = count > 0.5
    sub = iota((128, 128), 0)
    rank = dot(onehot(iota((128, 128), 1) < sub), onehot(present))
    table = jnp.zeros((8, 128), F32)
    for slot in range(CAP):
        hit = jnp.where(
            jnp.logical_and(present, rank == float(slot)), (sub + 1).astype(F32), 0.0
        )
        found = jnp.sum(hit, axis=0, keepdims=True) - 1.0
        table = jnp.where(iota((8, 128), 0) == slot, found, table)
    tabs[0] = table

    load_p.wait()
    raw = pv[...].astype(F32)
    pinv = 1.0 / jnp.sqrt(jnp.sum(raw * raw, axis=1, keepdims=True) + EPS)
    hat[pl.ds(own, PB), :] = (raw * pinv).astype(BF16)
    pl.semaphore_wait(barrier, 11)

    def own_send(cq):
        for name in ("x", "m0", "p0", "s00"):
            if cq >= 2:
                ag[name, cq - 2].wait_send()
                gone.add((name, cq - 2))
            ag[name, cq].start()

    gone = set()
    own_send(0)

    ask = []
    for rel in range(1, 8):
        to = inv_rel(rel)
        ask.append(remote(tabs.at[0], tabs.at[to], tab_s.at[rel], tab_r.at[to], partner[rel]))
        ask[-1].start()

    load_q.wait()

    def norm_rows(i, carry):
        rows = pl.ds(pl.multiple_of(i * 32, 32), 32)
        values = qv[rows, :].astype(F32)
        inverse = 1.0 / jnp.sqrt(jnp.sum(values * values, axis=1, keepdims=True) + EPS)
        qinv[rows, :] = jnp.broadcast_to(inverse, (32, 128))
        qhat[rows, :] = (values * inverse).astype(BF16)
        return carry

    def norm_queries(first, last):
        lax.fori_loop(first, last, norm_rows, 0)

    def build_selection():
        everything = tabs[...].reshape(64, 128).astype(BF16)
        lane = iota((128, 128), 1)
        who, o, slot = lane >> 4, (lane >> 2) & 3, lane & 3
        back_rel = ((4 - (who >> 1)) & 3) * 2 + (who & 1)
        flip = (who & 1) & ((who >> 1) & 1)
        diag = iota((64, 128), 0) == (who * 8 + slot)[:64]
        for j in range(4):
            theirs = jnp.where(flip == 1, (0, 2, 1, 3)[j], j)
            offset = (o >> 1) * 128 + ((o & 1) ^ (flip if j in (0, 3) else 0)) * 64
            pick = onehot(iota((128, 128), 0) == back_rel * 16 + theirs * 4 + o)
            local = jnp.sum(jnp.where(diag, dot(everything, pick), 0.0), axis=0, keepdims=True)
            target = jnp.where(local >= 0.0, local + offset[:1].astype(F32), -1.0)
            match = jnp.where(iota((CH, SL), 0).astype(F32) == target, 1.0, 0.0)
            selt[pl.ds(j * CH, CH), :] = match.astype(BF16)
            sel[pl.ds(j * SL, SL), :] = jnp.transpose(match).astype(BF16)

    def build_mask():
        lane = iota((128, Q), 1)
        from_lane = ((lane >> 4) & 7) * 16 + (lane >> 7) * 4 + ((lane >> 2) & 3)
        spread = dot(table.astype(BF16), onehot(iota((128, Q), 0) == from_lane))
        local = jnp.sum(
            jnp.where(iota((8, Q), 0) == (lane & 3)[:8], spread, 0.0), axis=0, keepdims=True
        )
        wanted = jnp.where(local >= 0.0, from_lane[:1] * 64 + local.astype(jnp.int32), -1)

        def rows_mask(i, carry):
            rows = pl.ds(pl.multiple_of(i * 64, 64), 64)
            mine = key_ref[rows, :]
            found = mine[:, 0:1] == wanted
            for h in range(1, HARD):
                found = jnp.logical_or(found, mine[:, h : h + 1] == wanted)
            exp_h[rows, :] = jnp.where(found, 1.0, 0.0)
            return carry

        lax.fori_loop(0, Q // 64, rows_mask, 0)

    def select(j, cq):
        def tile(n, carry):
            at = pl.ds(pl.multiple_of(cq * PW + n * TN, TN), TN)
            rows = dot(sel[pl.ds(j * SL, SL), :], hat[pl.ds(j * CH, CH), at]).astype(BF16)
            fsend[pl.ds(j * SL, SL), at] = rows
            fetched[pl.ds(j * SL, 16), at] = rows[:16]
            return carry

        lax.fori_loop(0, PW // TN, tile, 0)
        for rel in range(1, 8):
            fetch[j, cq, rel].start()

    totals = {"cycle": jnp.zeros((Q, 1), F32), "pos": jnp.zeros((Q, 1), F32)}

    def cycle_scores(j):
        scores = SCALE * lax.dot_general(
            qhat[...], hat[pl.ds(j * CH, CH), :], NT, preferred_element_type=F32
        )
        raised = jnp.exp(scores)
        exp_c[:, pl.ds(j * CH, CH)] = raised
        positive = kk_ref[...] == iota((Q, CH), 1) + j * CH
        totals["cycle"] = totals["cycle"] + jnp.sum(raised, axis=1, keepdims=True)
        totals["pos"] = totals["pos"] + jnp.sum(
            jnp.where(positive, scores, 0.0), axis=1, keepdims=True
        )

    positives = pos_ref[...]
    chunk, o = place(lax.shift_right_logical(positives, 6))
    spots = chunk * CH + o * PB + (positives & 63)
    stacked = jnp.concatenate(
        [keys.astype(F32), jnp.broadcast_to(spots.astype(F32), (120, Q))], axis=0
    )
    turned = jnp.transpose(stacked).astype(jnp.int32)
    key_ref[...] = turned
    kk_ref[...] = turned[:, HARD : HARD + 1]

    def sib_relay(cq, *names):
        for came, sent in names:
            ag[came, cq].wait_recv()
            ag[sent, cq].start()

    def z_relay(dxh, cq):
        ag[f"t{dxh}", cq].start()

    def from_sib(cq, *names):
        for name in names:
            ag[name, cq].wait_recv()

    own_send(1)
    norm_queries(0, 4)
    for copy in ask:
        copy.wait_recv()
    build_selection()
    for cq in ALL_PARTS:
        sib_relay(cq, ("x", "s01"), ("m0", "s30"), ("p0", "s10"))
        if cq + 2 < PARTS:
            own_send(cq + 2)
        if cq > 0:
            ag["m1", cq - 1].start()
            ag["p1", cq - 1].start()
        norm_queries(4 + 3 * cq, 7 + 3 * cq)
        from_sib(cq, "s00", "s01")
        select(0, cq)
        from_sib(cq, "s30", "s10")
        select(1, cq)
    ag["m1", PARTS - 1].start()
    ag["p1", PARTS - 1].start()
    for cq in ALL_PARTS:
        z_relay(0, cq)
    for cq in ALL_PARTS:
        sib_relay(cq, ("m1", "s31"), ("p1", "s11"))
        z_relay(1, cq)
        if cq < 2:
            cycle_scores(cq)
        from_sib(cq, "s31", "s11")
        select(2, cq)
    for cq in ALL_PARTS:
        sib_relay(cq, ("t0", "s20"), ("t1", "s21"))
        if cq == 0:
            cycle_scores(2)
        from_sib(cq, "s20", "s21")
        select(3, cq)
    cycle_scores(3)
    build_mask()

    pos_score = totals["pos"]
    pos_exp = jnp.exp(pos_score)
    hard_total = pos_exp
    for step in ((0, 1, 2), (3,)):
        for j in step:
            for cq in ALL_PARTS:
                for rel in range(1, 8):
                    fetch[j, cq, rel].wait_recv()
        at = pl.ds(step[0] * SL, len(step) * SL)
        scores = SCALE * lax.dot_general(
            qhat[...], fetched[at, :], NT, preferred_element_type=F32
        )
        raised = exp_h[:, at] * jnp.exp(scores)
        exp_h[:, at] = raised
        hard_total = hard_total + jnp.sum(raised, axis=1, keepdims=True)
    for copy in fetch.values():
        copy.wait_send()
    hard_inv = 1.0 / hard_total

    def back_sums(first, chunks, parts=ALL_PARTS):
        slots = pl.ds(first * SL, chunks * SL)

        def tile(n, carry):
            at = pl.ds(pl.multiple_of(n * TN, TN), TN)
            rows = (SCALE * dot(wht[slots, :], qhat[:, at])).astype(BF16)
            fsend[slots, at] = rows
            for i in range(chunks):
                sret[pl.ds((first + i) * SL, 16), at] = rows[i * SL : i * SL + 16]
            return carry

        lax.fori_loop(parts[0] * PW // TN, (parts[-1] + 1) * PW // TN, tile, 0)

    def hard_weights(first, chunks):
        slots = pl.ds(first * SL, chunks * SL)
        weights = exp_h[:, slots] * hard_inv
        wh[:, slots] = weights.astype(BF16)
        wht[slots, :] = jnp.transpose(weights).astype(BF16)

    left = set()

    def back_start(step):
        j, cq = BWD_STEPS[step]
        for rel in range(1, 8):
            if step >= DEPTH:
                earlier = BWD_STEPS[step - DEPTH] + (rel,)
                back[earlier].wait_send()
                left.add(earlier)
            back[j, cq, rel].start()

    hard_weights(3, 1)
    back_sums(3, 1, ALL_PARTS[:1])
    back_start(0)
    back_sums(3, 1, ALL_PARTS[1:])
    back_start(1)
    hard_weights(0, 3)
    back_sums(0, 3)
    for step in range(2, DEPTH):
        back_start(step)

    cycle_total = totals["cycle"]
    losses = jnp.log(cycle_total) + jnp.log(hard_total) - 2.0 * pos_score
    for i in range(Q // 128):
        spread = jnp.broadcast_to(losses[i * 128 : (i + 1) * 128], (128, 128))
        out_l[pl.ds(i, 1), :] = jnp.transpose(spread)[:1]
    cycle_inv = 1.0 / cycle_total
    correction = 2.0 - pos_exp * hard_inv
    for j in (3, 2, 1, 0):
        at = pl.ds(j * CH, CH)
        positive = kk_ref[...] == iota((Q, CH), 1) + j * CH
        weights = exp_c[:, at] * cycle_inv - jnp.where(positive, correction, 0.0)
        wc[:, at] = weights.astype(BF16)
        wct[at, :] = jnp.transpose(weights).astype(BF16)

    QR = 256
    store_q = []
    along_q = {}

    def query_tiles(block, first, last):
        rows = pl.ds(block * QR, QR)
        inverse = qinv[rows, 0:1]

        def product(n, total):
            at = pl.ds(pl.multiple_of(n * TN, TN), TN)
            tile = SCALE * (dot(wc[rows, :], hat[:, at]) + dot(wh[rows, :], fetched[:, at]))
            qsum[:, at] = tile
            unit = qv[rows, at].astype(F32) * inverse
            return total + jnp.sum(unit * tile, axis=1, keepdims=True)

        start = along_q.get(block, jnp.zeros((QR, 1), F32))
        along_q[block] = lax.fori_loop(first, last, product, start)

    def query_store(block):
        rows = pl.ds(block * QR, QR)
        inverse = qinv[rows, 0:1]
        along = along_q[block]

        def project(n, carry):
            at = pl.ds(pl.multiple_of(n * TN, TN), TN)
            unit = qv[rows, at].astype(F32) * inverse
            qv[rows, at] = ((qsum[:, at] - unit * along) * inverse).astype(BF16)
            return carry

        lax.fori_loop(0, D // TN, project, 0)
        store_q.append(
            pltpu.make_async_copy(qv.at[rows, :], out_q.at[rows, :], lsem.at[2 + block])
        )
        store_q[-1].start()

    def query_work(i):
        block, piece = i // 3, i % 3
        if piece < 2:
            query_tiles(block, piece * 4, piece * 4 + 4)
        else:
            query_store(block)

    def partial(j, cq):
        for rel in range(1, 8):
            back[j, cq, rel].wait_recv()

        def tile(n, carry):
            at = pl.ds(pl.multiple_of(cq * PW + n * TN, TN), TN)
            total = SCALE * dot(wct[pl.ds(j * CH, CH), :], qhat[:, at]) + dot(
                selt[pl.ds(j * CH, CH), :], sret[pl.ds(j * SL, SL), at]
            )
            part[pl.ds(j * CH, CH), at] = total.astype(BF16)
            return carry

        lax.fori_loop(0, PW // TN, tile, 0)
        rs["sib", j, cq].start()

    def reduce(j, cq):
        at = cols(cq)
        mine = pl.ds(j * CH, SL)
        rs["sib", j, cq].wait_recv()
        total = part[mine, at].astype(F32) + sibr[pl.ds(j * SL, SL), at].astype(F32)
        if j == 3:
            part[mine, at] = total.astype(BF16)
            rs["z", 3, cq].start()
        elif j > 0:
            here = pl.ds((j - 1) * PB, PB)
            rs["z", 3, cq].wait_recv() if j == 2 else None
            more = z2[here, at].astype(F32)
            first, second = total[:PB], total[PB:]
            if cq < HALF:
                first = first + more
            else:
                second = second + more
            part[pl.ds(j * CH, PB), at] = first.astype(BF16)
            rs["zp", j, cq].start()
            part[pl.ds(j * CH + PB, PB), at] = second.astype(BF16)
            rs["zm", j, cq].start()
        else:
            for dxh in (1, 0):
                rs["zp", 1 + dxh, cq].wait_recv()
                rs["zm", 1 + dxh, cq].wait_recv()
                here = pl.ds(dxh * PB, PB)
                both = z1m[here, at].astype(F32) + z1p[here, at].astype(F32)
                both = both + total[dxh * PB : (dxh + 1) * PB]
                if dxh == 1:
                    part[here, at] = both.astype(BF16)
                    rs["x", cq].start()
                else:
                    qsum[:PB, at] = both

    waiting = []
    for step, (j, cq) in enumerate(BWD_STEPS):
        partial(j, cq)
        if step + DEPTH < STEPS:
            back_start(step + DEPTH)
        waiting.append((j, cq))
        if len(waiting) > 1:
            reduce(*waiting.pop(0))
        if 1 <= step <= 6:
            query_work(step - 1)
    reduce(*waiting.pop(0))

    unit = pv[...].astype(F32) * pinv
    for cq in ALL_PARTS:
        rs["x", cq].wait_recv()
    total = qsum[:PB, :] + xr[...].astype(F32)
    along = jnp.sum(unit * total, axis=1, keepdims=True)
    out_p[...] = ((total - unit * along) * pinv).astype(BF16)

    for key, copy in ag.items():
        if key not in gone:
            copy.wait_send()
    for copy in ask + list(rs.values()):
        copy.wait_send()
    for key, copy in back.items():
        if key not in left:
            copy.wait_send()
    for copy in store_q:
        copy.wait()


def hand_over(in_q, in_p, in_l, out_q, out_p, out_l, hold_q, hold_p, hold_l, sem_in, sem_out):
    pieces = [(in_p, hold_p, out_p), (in_l, hold_l, out_l)]
    for i in range(8):
        rows = pl.ds(i * (Q // 8), Q // 8)
        pieces.append((in_q.at[rows, :], hold_q.at[rows, :], out_q.at[rows, :]))
    loads, stores = [], []
    for i, (source, hold, target) in enumerate(pieces):
        loads.append(pltpu.make_async_copy(source, hold, sem_in.at[i]))
        stores.append(pltpu.make_async_copy(hold, target, sem_out.at[i]))
    for load in loads:
        load.start()
    for load, store in zip(loads, stores):
        load.wait()
        store.start()
    for store in stores:
        store.wait()


def shards(queries, passages, positives, hard_ids):
    dma = pltpu.SemaphoreType.DMA
    any_spec = pl.BlockSpec(memory_space=pl.ANY)
    vmem_spec = pl.BlockSpec(memory_space=pltpu.VMEM)
    query_grads, passage_grads, losses = pl.pallas_call(
        kernel,
        out_shape=(
            jax.ShapeDtypeStruct((Q, D), BF16),
            jax.ShapeDtypeStruct((PB, D), BF16),
            jax.ShapeDtypeStruct((Q // 128, 128), F32),
        ),
        in_specs=[any_spec, any_spec, vmem_spec, vmem_spec],
        out_specs=(any_spec, vmem_spec, vmem_spec),
        scratch_shapes=[
            pltpu.VMEM((PB, D), BF16),
            pltpu.VMEM((Q, D), BF16),
            pltpu.VMEM((Q, D), BF16),
            pltpu.VMEM((4 * CH, D), BF16),
            pltpu.VMEM((4 * SL, D), BF16),
            pltpu.VMEM((4 * SL, D), BF16),
            pltpu.VMEM((4 * SL, D), BF16),
            pltpu.VMEM((4 * CH, D), BF16),
            pltpu.VMEM((4 * SL, D), BF16),
            pltpu.VMEM((SL, D), BF16),
            pltpu.VMEM((SL, D), BF16),
            pltpu.VMEM((SL, D), BF16),
            pltpu.VMEM((PB, D), BF16),
            pltpu.VMEM((Q, 4 * CH), F32),
            pltpu.VMEM((Q, 4 * SL), F32),
            pltpu.VMEM((Q, 4 * CH), BF16),
            pltpu.VMEM((4 * CH, Q), BF16),
            pltpu.VMEM((Q, 4 * SL), BF16),
            pltpu.VMEM((4 * SL, Q), BF16),
            pltpu.VMEM((256, D), F32),
            pltpu.VMEM((4 * SL, CH), BF16),
            pltpu.VMEM((4 * CH, SL), BF16),
            pltpu.VMEM((8, 8, 128), F32),
            pltpu.VMEM((Q, 128), F32),
            pltpu.VMEM((Q, 128), jnp.int32),
            pltpu.VMEM((Q, 1), jnp.int32),
            dma((8,)),
            dma((15 * PARTS,)), dma((15 * PARTS,)),
            dma((8,)), dma((8,)),
            dma((STEPS, 8)), dma((STEPS, 8)),
            dma((STEPS, 8)), dma((STEPS, 8)),
            dma((10 * PARTS,)), dma((10 * PARTS,)),
        ],
        compiler_params=pltpu.CompilerParams(
            collective_id=0, has_side_effects=True, vmem_limit_bytes=63 * 2**20
        ),
        cost_estimate=pl.CostEstimate(
            flops=6 * Q * 1536 * D, bytes_accessed=4 * Q * D, transcendentals=Q * 1536
        ),
    )(passages, queries, hard_ids.T, positives.reshape(1, Q))
    query_grads, passage_grads, losses = pl.pallas_call(
        hand_over,
        out_shape=(
            jax.ShapeDtypeStruct((Q, D), BF16),
            jax.ShapeDtypeStruct((PB, D), BF16),
            jax.ShapeDtypeStruct((Q // 128, 128), F32),
        ),
        in_specs=[any_spec] * 3,
        out_specs=(any_spec,) * 3,
        scratch_shapes=[
            pltpu.VMEM((Q, D), BF16),
            pltpu.VMEM((PB, D), BF16),
            pltpu.VMEM((Q // 128, 128), F32),
            dma((10,)),
            dma((10,)),
        ],
        compiler_params=pltpu.CompilerParams(vmem_limit_bytes=63 * 2**20),
        cost_estimate=pl.CostEstimate(flops=0, bytes_accessed=4 * Q * D, transcendentals=0),
    )(query_grads, passage_grads, losses)
    return query_grads, passage_grads, losses.reshape(Q)


def solution(mesh):
    in_specs = (
        P(("blk", "group"), None),
        P(("blk", "group"), None),
        P(("blk", "group")),
        P(("blk", "group"), None),
    )
    out_specs = (P(("blk", "group"), None), P(("blk", "group"), None), P(("blk", "group")))
    return jax.shard_map(shards, mesh=mesh, in_specs=in_specs, out_specs=out_specs, check_vma=False)
```

```python
import jax
import jax.numpy as jnp
from jax import lax
from jax.experimental import pallas as pl
from jax.experimental.pallas import tpu as pltpu
from jax.sharding import PartitionSpec as P

D = 4096
Q = 512
PB = 64
HARD = 8
CAP = 4
SCALE = 20.0
EPS = 1e-06
CH = 256
SL = 128
PARTS = 4
PW = D // PARTS
TN = 512
HALF = PARTS // 2
ALL_PARTS = tuple(range(PARTS))
AHEAD = (4,) * 16
STEPS = 4 * PARTS
BWD_STEPS = tuple((j, cq) for j in (3, 2, 1, 0) for cq in ALL_PARTS)
MESH = pl.DeviceIdType.MESH
F32 = jnp.float32
BF16 = jnp.bfloat16
NT = (((1,), (1,)), ((), ()))
TN_DIMS = (((0,), (0,)), ((), ()))


def iota(shape, dim):
    return lax.broadcasted_iota(jnp.int32, shape, dim)


def inv_rel(rel):
    return ((4 - rel // 2) % 4) * 2 + rel % 2


def flips(rel):
    return (rel % 2) & (rel // 2 % 2)


def seen_by(rel, j):
    return (0, 2, 1, 3)[j] if flips(rel) else j


def dot(a, b):
    return jnp.dot(a, b, preferred_element_type=F32)


def onehot(mask):
    return jnp.where(mask, 1.0, 0.0).astype(BF16)


def kernel(
    passages, queries, ids_ref, pos_ref, out_q, out_p, out_l,
    pv, qv, qhat, hat, fsend, fetched, sret, part, sibr, z2, z1m, z1p, xr,
    exp_c, exp_h, wc, wct, wh, wht, qsum, sel, selt, tabs, qinv, key_ref, kk_ref,
    lsem, ag_s, ag_r, tab_s, tab_r, f_s, f_r, r_s, r_r, rs_s, rs_r,
):
    blk = lax.axis_index("blk")
    grp = lax.axis_index("group")
    xh, z, core = blk // 8, (blk // 2) % 4, blk % 2
    y, xl = grp // 2, grp % 2

    def dev(dxh=0, dz=0, dc=0, dy=0, dxl=0):
        return (
            ((xh + dxh) % 2) * 8 + ((z + dz) % 4) * 2 + (core + dc) % 2,
            ((y + dy) % 4) * 2 + (xl + dxl) % 2,
        )

    sib, zp, zm, xo = dev(dc=1), dev(dz=1), dev(dz=3), dev(dxh=1)
    partner = [
        dev(dy=rel // 2, dxl=rel % 2, dxh=flips(rel)) for rel in range(8)
    ]

    barrier = pltpu.get_barrier_semaphore()
    for d in [sib, zp, zm, xo] + partner[1:]:
        pl.semaphore_signal(barrier, inc=1, device_id=d, device_id_type=MESH)

    load_p = pltpu.make_async_copy(passages, pv, lsem.at[0])
    load_q = pltpu.make_async_copy(queries, qv, lsem.at[1])
    load_p.start()
    load_q.start()

    def remote(src, dst, ss, rs, d):
        return pltpu.make_async_remote_copy(
            src_ref=src, dst_ref=dst, send_sem=ss, recv_sem=rs, device_id=d, device_id_type=MESH
        )

    def cols(part_id):
        return pl.ds(part_id * PW, PW)

    ag = {}

    def row(dz, dc, dxh):
        chunk, side = (1 + dxh, dz // 2) if dz % 2 else (dz // 2 * 3, dxh)
        return chunk * CH + dc * 2 * PB + side * PB

    def add_ag(name, src, dst, d, parts=ALL_PARTS):
        for cq in parts:
            i = len(ag)
            ag[name, cq] = remote(
                hat.at[pl.ds(src, PB), cols(cq)], hat.at[pl.ds(dst, PB), cols(cq)],
                ag_s.at[i], ag_r.at[i], d,
            )

    own = row(0, 0, 0)
    add_ag("x", own, row(0, 0, 1), xo)
    add_ag("m0", own, row(3, 0, 0), zp)
    add_ag("p0", own, row(1, 0, 0), zm)
    add_ag("s00", own, row(0, 1, 0), sib)
    add_ag("s01", row(0, 0, 1), row(0, 1, 1), sib)
    add_ag("m1", row(0, 0, 1), row(3, 0, 1), zp)
    add_ag("p1", row(0, 0, 1), row(1, 0, 1), zm)
    for dxh in range(2):
        add_ag(f"s3{dxh}", row(3, 0, dxh), row(3, 1, dxh), sib)
        add_ag(f"s1{dxh}", row(1, 0, dxh), row(1, 1, dxh), sib)
        add_ag(f"t{dxh}", row(3, 0, dxh), row(2, 0, dxh), zp, ALL_PARTS[:HALF])
        add_ag(f"t{dxh}", row(1, 0, dxh), row(2, 0, dxh), zm, ALL_PARTS[HALF:])
        add_ag(f"s2{dxh}", row(2, 0, dxh), row(2, 1, dxh), sib)

    fetch, back = {}, {}
    for step, (j, cq) in enumerate(BWD_STEPS):
        for rel in range(1, 8):
            to, theirs = inv_rel(rel), seen_by(rel, j)
            fetch[j, cq, rel] = remote(
                fsend.at[pl.ds(j * SL + rel * 16, 16), cols(cq)],
                fetched.at[pl.ds(theirs * SL + to * 16, 16), cols(cq)],
                f_s.at[step, rel], f_r.at[step, to], partner[rel],
            )
            back[j, cq, rel] = remote(
                fsend.at[pl.ds(theirs * SL + rel * 16, 16), cols(cq)],
                sret.at[pl.ds(j * SL + to * 16, 16), cols(cq)],
                r_s.at[step, rel], r_r.at[step, to], partner[rel],
            )

    rs = {}

    def add_rs(name, src, dst, d):
        i = len(rs)
        rs[name] = remote(src, dst, rs_s.at[i], rs_r.at[i], d)

    for j, cq in BWD_STEPS:
        add_rs(
            ("sib", j, cq),
            part.at[pl.ds(j * CH + SL, SL), cols(cq)], sibr.at[pl.ds(j * SL, SL), cols(cq)], sib,
        )
    for cq in ALL_PARTS:
        add_rs(
            ("z", 3, cq),
            part.at[pl.ds(3 * CH, SL), cols(cq)], z2.at[:, cols(cq)], zp if cq < HALF else zm,
        )
        for j in (2, 1):
            there = pl.ds((j - 1) * PB, PB)
            add_rs(
                ("zp", j, cq), part.at[pl.ds(j * CH, PB), cols(cq)], z1m.at[there, cols(cq)], zp
            )
            add_rs(
                ("zm", j, cq), part.at[pl.ds(j * CH + PB, PB), cols(cq)], z1p.at[there, cols(cq)], zm
            )
        add_rs(("x", cq), part.at[pl.ds(PB, PB), cols(cq)], xr.at[:, cols(cq)], xo)

    def place(block):
        dz = (lax.shift_right_logical(block, 1) - z) & 3
        dxh = lax.shift_right_logical(block, 3) ^ xh
        odd, far = (dz & 1) == 1, lax.shift_right_logical(dz, 1)
        chunk, side = jnp.where(odd, 1 + dxh, 3 * far), jnp.where(odd, far, dxh)
        return chunk, ((block & 1) ^ core) * 2 + side

    ids = ids_ref[...]
    owner = lax.shift_right_logical(ids, 6)
    og = owner & 7
    rel_g = ((lax.shift_right_logical(og, 1) - y) & 3) * 2 + ((og & 1) ^ xl)
    chunk, o = place(lax.shift_right_logical(owner, 3))
    keys = (rel_g * 16 + chunk * 4 + o) * 64 + (ids & 63)
    count = jnp.zeros((128, 128), F32)
    sub_q = iota((128, Q), 0)
    for h in range(HARD):
        key = keys[h : h + 1]
        hi = onehot(lax.shift_right_logical(key, 6) == sub_q)
        lo = onehot((key & 63) == sub_q)
        count = count + lax.dot_general(lo, hi, NT, preferred_element_type=F32)
    present = count > 0.5
    sub = iota((128, 128), 0)
    rank = dot(onehot(iota((128, 128), 1) < sub), onehot(present))
    table = jnp.zeros((8, 128), F32)
    for slot in range(CAP):
        hit = jnp.where(
            jnp.logical_and(present, rank == float(slot)), (sub + 1).astype(F32), 0.0
        )
        found = jnp.sum(hit, axis=0, keepdims=True) - 1.0
        table = jnp.where(iota((8, 128), 0) == slot, found, table)
    tabs[0] = table

    load_p.wait()
    raw = pv[...].astype(F32)
    pinv = 1.0 / jnp.sqrt(jnp.sum(raw * raw, axis=1, keepdims=True) + EPS)
    hat[pl.ds(own, PB), :] = (raw * pinv).astype(BF16)
    pl.semaphore_wait(barrier, 11)

    def own_send(cq):
        for name in ("x", "m0", "p0", "s00"):
            if cq >= 2:
                ag[name, cq - 2].wait_send()
                gone.add((name, cq - 2))
            ag[name, cq].start()

    gone = set()
    own_send(0)

    ask = []
    for rel in range(1, 8):
        to = inv_rel(rel)
        ask.append(remote(tabs.at[0], tabs.at[to], tab_s.at[rel], tab_r.at[to], partner[rel]))
        ask[-1].start()

    load_q.wait()

    def norm_rows(i, carry):
        rows = pl.ds(pl.multiple_of(i * 32, 32), 32)
        values = qv[rows, :].astype(F32)
        inverse = 1.0 / jnp.sqrt(jnp.sum(values * values, axis=1, keepdims=True) + EPS)
        qinv[rows, :] = jnp.broadcast_to(inverse, (32, 128))
        qhat[rows, :] = (values * inverse).astype(BF16)
        return carry

    def norm_queries(first, last):
        lax.fori_loop(first, last, norm_rows, 0)

    def build_selection():
        everything = tabs[...].reshape(64, 128).astype(BF16)
        lane = iota((128, 128), 1)
        who, o, slot = lane >> 4, (lane >> 2) & 3, lane & 3
        back_rel = ((4 - (who >> 1)) & 3) * 2 + (who & 1)
        flip = (who & 1) & ((who >> 1) & 1)
        diag = iota((64, 128), 0) == (who * 8 + slot)[:64]
        for j in range(4):
            theirs = jnp.where(flip == 1, (0, 2, 1, 3)[j], j)
            offset = (o >> 1) * 128 + ((o & 1) ^ (flip if j in (0, 3) else 0)) * 64
            pick = onehot(iota((128, 128), 0) == back_rel * 16 + theirs * 4 + o)
            local = jnp.sum(jnp.where(diag, dot(everything, pick), 0.0), axis=0, keepdims=True)
            target = jnp.where(local >= 0.0, local + offset[:1].astype(F32), -1.0)
            match = jnp.where(iota((CH, SL), 0).astype(F32) == target, 1.0, 0.0)
            selt[pl.ds(j * CH, CH), :] = match.astype(BF16)
            sel[pl.ds(j * SL, SL), :] = jnp.transpose(match).astype(BF16)

    def build_mask():
        lane = iota((128, Q), 1)
        from_lane = ((lane >> 4) & 7) * 16 + (lane >> 7) * 4 + ((lane >> 2) & 3)
        spread = dot(table.astype(BF16), onehot(iota((128, Q), 0) == from_lane))
        local = jnp.sum(
            jnp.where(iota((8, Q), 0) == (lane & 3)[:8], spread, 0.0), axis=0, keepdims=True
        )
        wanted = jnp.where(local >= 0.0, from_lane[:1] * 64 + local.astype(jnp.int32), -1)

        def rows_mask(i, carry):
            rows = pl.ds(pl.multiple_of(i * 64, 64), 64)
            mine = key_ref[rows, :]
            found = mine[:, 0:1] == wanted
            for h in range(1, HARD):
                found = jnp.logical_or(found, mine[:, h : h + 1] == wanted)
            exp_h[rows, :] = jnp.where(found, 1.0, 0.0)
            return carry

        lax.fori_loop(0, Q // 64, rows_mask, 0)

    def select(j, cq):
        def tile(n, carry):
            at = pl.ds(pl.multiple_of(cq * PW + n * TN, TN), TN)
            rows = dot(sel[pl.ds(j * SL, SL), :], hat[pl.ds(j * CH, CH), at]).astype(BF16)
            fsend[pl.ds(j * SL, SL), at] = rows
            fetched[pl.ds(j * SL, 16), at] = rows[:16]
            return carry

        lax.fori_loop(0, PW // TN, tile, 0)
        for rel in range(1, 8):
            fetch[j, cq, rel].start()

    totals = {"cycle": jnp.zeros((Q, 1), F32), "pos": jnp.zeros((Q, 1), F32)}

    def cycle_scores(j):
        scores = SCALE * lax.dot_general(
            qhat[...], hat[pl.ds(j * CH, CH), :], NT, preferred_element_type=F32
        )
        raised = jnp.exp(scores)
        exp_c[:, pl.ds(j * CH, CH)] = raised
        positive = kk_ref[...] == iota((Q, CH), 1) + j * CH
        totals["cycle"] = totals["cycle"] + jnp.sum(raised, axis=1, keepdims=True)
        totals["pos"] = totals["pos"] + jnp.sum(
            jnp.where(positive, scores, 0.0), axis=1, keepdims=True
        )

    positives = pos_ref[...]
    chunk, o = place(lax.shift_right_logical(positives, 6))
    spots = chunk * CH + o * PB + (positives & 63)
    stacked = jnp.concatenate(
        [keys.astype(F32), jnp.broadcast_to(spots.astype(F32), (120, Q))], axis=0
    )
    turned = jnp.transpose(stacked).astype(jnp.int32)
    key_ref[...] = turned
    kk_ref[...] = turned[:, HARD : HARD + 1]

    def sib_relay(cq, *names):
        for came, sent in names:
            ag[came, cq].wait_recv()
            ag[sent, cq].start()

    def z_relay(dxh, cq):
        ag[f"t{dxh}", cq].start()

    def from_sib(cq, *names):
        for name in names:
            ag[name, cq].wait_recv()

    own_send(1)
    norm_queries(0, 4)
    own_send(2)
    for copy in ask:
        copy.wait_recv()
    build_selection()
    own_send(3)
    for cq in ALL_PARTS:
        sib_relay(cq, ("x", "s01"), ("m0", "s30"), ("p0", "s10"))
        ag["m1", cq].start()
        ag["p1", cq].start()
        z_relay(0, cq)
        norm_queries(4 + 3 * cq, 7 + 3 * cq)
        from_sib(cq, "s00", "s01")
        select(0, cq)
        from_sib(cq, "s30", "s10")
        select(1, cq)
    for cq in ALL_PARTS:
        sib_relay(cq, ("m1", "s31"), ("p1", "s11"))
        z_relay(1, cq)
        from_sib(cq, "s31", "s11")
        select(2, cq)
    for j in range(3):
        cycle_scores(j)
    for cq in ALL_PARTS:
        sib_relay(cq, ("t0", "s20"), ("t1", "s21"))
    for cq in ALL_PARTS:
        from_sib(cq, "s20", "s21")
        select(3, cq)
    cycle_scores(3)
    build_mask()

    pos_score = totals["pos"]
    pos_exp = jnp.exp(pos_score)
    hard_total = pos_exp
    for (j, cq, rel), copy in fetch.items():
        if j != 3:
            copy.wait_send()
    for step in ((0, 1, 2), (3,)):
        for j in step:
            for cq in ALL_PARTS:
                for rel in range(1, 8):
                    fetch[j, cq, rel].wait_recv()
        at = pl.ds(step[0] * SL, len(step) * SL)
        scores = SCALE * lax.dot_general(
            qhat[...], fetched[at, :], NT, preferred_element_type=F32
        )
        raised = exp_h[:, at] * jnp.exp(scores)
        exp_h[:, at] = raised
        hard_total = hard_total + jnp.sum(raised, axis=1, keepdims=True)
    for (j, cq, rel), copy in fetch.items():
        if j == 3:
            copy.wait_send()
    hard_inv = 1.0 / hard_total

    def back_sums(first, chunks, parts=ALL_PARTS):
        slots = pl.ds(first * SL, chunks * SL)

        def tile(n, carry):
            at = pl.ds(pl.multiple_of(n * TN, TN), TN)
            rows = (SCALE * dot(wht[slots, :], qhat[:, at])).astype(BF16)
            fsend[slots, at] = rows
            for i in range(chunks):
                sret[pl.ds((first + i) * SL, 16), at] = rows[i * SL : i * SL + 16]
            return carry

        lax.fori_loop(parts[0] * PW // TN, (parts[-1] + 1) * PW // TN, tile, 0)

    def hard_weights(first, chunks):
        slots = pl.ds(first * SL, chunks * SL)
        weights = exp_h[:, slots] * hard_inv
        wh[:, slots] = weights.astype(BF16)
        wht[slots, :] = jnp.transpose(weights).astype(BF16)

    left = set()

    def back_start(step):
        j, cq = BWD_STEPS[step]
        for rel in range(1, 8):
            earlier = BWD_STEPS[max(step - AHEAD[step], 0)] + (rel,)
            if step >= AHEAD[step] and earlier not in left:
                back[earlier].wait_send()
                left.add(earlier)
            back[j, cq, rel].start()

    hard_weights(3, 1)
    back_sums(3, 1, ALL_PARTS[:1])
    back_start(0)
    back_sums(3, 1, ALL_PARTS[1:])
    back_start(1)
    hard_weights(0, 3)
    back_sums(0, 3)
    for step in range(2, AHEAD[0]):
        back_start(step)

    cycle_total = totals["cycle"]
    losses = jnp.log(cycle_total) + jnp.log(hard_total) - 2.0 * pos_score
    for i in range(Q // 128):
        spread = jnp.broadcast_to(losses[i * 128 : (i + 1) * 128], (128, 128))
        out_l[pl.ds(i, 1), :] = jnp.transpose(spread)[:1]
    cycle_inv = 1.0 / cycle_total
    correction = 2.0 - pos_exp * hard_inv
    for j in (3, 2, 1, 0):
        at = pl.ds(j * CH, CH)
        positive = kk_ref[...] == iota((Q, CH), 1) + j * CH
        weights = exp_c[:, at] * cycle_inv - jnp.where(positive, correction, 0.0)
        wc[:, at] = weights.astype(BF16)
        wct[at, :] = jnp.transpose(weights).astype(BF16)

    QR = 256
    store_q = []
    along_q = {}

    def query_tiles(block, first, last):
        rows = pl.ds(block * QR, QR)
        inverse = qinv[rows, 0:1]

        def product(n, total):
            at = pl.ds(pl.multiple_of(n * TN, TN), TN)
            tile = SCALE * (dot(wc[rows, :], hat[:, at]) + dot(wh[rows, :], fetched[:, at]))
            qsum[:, at] = tile
            unit = qv[rows, at].astype(F32) * inverse
            return total + jnp.sum(unit * tile, axis=1, keepdims=True)

        start = along_q.get(block, jnp.zeros((QR, 1), F32))
        along_q[block] = lax.fori_loop(first, last, product, start)

    def query_store(block):
        rows = pl.ds(block * QR, QR)
        inverse = qinv[rows, 0:1]
        along = along_q[block]

        def project(n, carry):
            at = pl.ds(pl.multiple_of(n * TN, TN), TN)
            unit = qv[rows, at].astype(F32) * inverse
            qv[rows, at] = ((qsum[:, at] - unit * along) * inverse).astype(BF16)
            return carry

        lax.fori_loop(0, D // TN, project, 0)
        store_q.append(
            pltpu.make_async_copy(qv.at[rows, :], out_q.at[rows, :], lsem.at[2 + block])
        )
        store_q[-1].start()

    def query_work(i):
        block, piece = i // 3, i % 3
        if piece < 2:
            query_tiles(block, piece * 4, piece * 4 + 4)
        else:
            query_store(block)

    def partial(j, cq):
        def tile(n, carry):
            at = pl.ds(pl.multiple_of(cq * PW + n * TN, TN), TN)
            total = SCALE * dot(wct[pl.ds(j * CH, CH), :], qhat[:, at]) + dot(
                selt[pl.ds(j * CH, CH), :], sret[pl.ds(j * SL, SL), at]
            )
            part[pl.ds(j * CH, CH), at] = total.astype(BF16)
            return carry

        lax.fori_loop(0, PW // TN, tile, 0)
        rs["sib", j, cq].start()

    def reduce(j, cq):
        at = cols(cq)
        mine = pl.ds(j * CH, SL)
        rs["sib", j, cq].wait_recv()
        total = part[mine, at].astype(F32) + sibr[pl.ds(j * SL, SL), at].astype(F32)
        if j == 3:
            part[mine, at] = total.astype(BF16)
            rs["z", 3, cq].start()
        elif j > 0:
            here = pl.ds((j - 1) * PB, PB)
            rs["z", 3, cq].wait_recv() if j == 2 else None
            more = z2[here, at].astype(F32)
            first, second = total[:PB], total[PB:]
            if cq < HALF:
                first = first + more
            else:
                second = second + more
            part[pl.ds(j * CH, PB), at] = first.astype(BF16)
            rs["zp", j, cq].start()
            part[pl.ds(j * CH + PB, PB), at] = second.astype(BF16)
            rs["zm", j, cq].start()
        else:
            for dxh in (1, 0):
                rs["zp", 1 + dxh, cq].wait_recv()
                rs["zm", 1 + dxh, cq].wait_recv()
                here = pl.ds(dxh * PB, PB)
                both = z1m[here, at].astype(F32) + z1p[here, at].astype(F32)
                both = both + total[dxh * PB : (dxh + 1) * PB]
                if dxh == 1:
                    part[here, at] = both.astype(BF16)
                    rs["x", cq].start()
                else:
                    qsum[:PB, at] = both

    for key, copy in ag.items():
        if key not in gone:
            copy.wait_send()
    for copy in ask:
        copy.wait_send()
    for i in range(3):
        query_work(i)
    waiting, started = [], AHEAD[0]
    for step, (j, cq) in enumerate(BWD_STEPS):
        for rel in range(1, 8):
            back[j, cq, rel].wait_recv()
        while started < STEPS and started - AHEAD[started] <= step:
            back_start(started)
            started += 1
        partial(j, cq)
        waiting.append((j, cq))
        while len(waiting) > (1 if step < 12 else 0):
            reduce(*waiting.pop(0))
        if step in (3, 5, 7):
            query_work(3 + (step - 3) // 2)

    for key, copy in back.items():
        if key not in left:
            copy.wait_send()
    for key, copy in rs.items():
        if key[0] != "x":
            copy.wait_send()
    for copy in store_q:
        copy.wait()
    unit = pv[...].astype(F32) * pinv
    for cq in ALL_PARTS:
        rs["x", cq].wait_recv()
    total = qsum[:PB, :] + xr[...].astype(F32)
    along = jnp.sum(unit * total, axis=1, keepdims=True)
    out_p[...] = ((total - unit * along) * pinv).astype(BF16)

    for cq in ALL_PARTS:
        rs["x", cq].wait_send()


def hand_over(in_q, in_p, in_l, out_q, out_p, out_l, hold_q, hold_p, hold_l, sem_in, sem_out):
    pieces = [(in_p, hold_p, out_p), (in_l, hold_l, out_l)]
    for i in range(8):
        rows = pl.ds(i * (Q // 8), Q // 8)
        pieces.append((in_q.at[rows, :], hold_q.at[rows, :], out_q.at[rows, :]))
    loads, stores = [], []
    for i, (source, hold, target) in enumerate(pieces):
        loads.append(pltpu.make_async_copy(source, hold, sem_in.at[i]))
        stores.append(pltpu.make_async_copy(hold, target, sem_out.at[i]))
    for load in loads:
        load.start()
    for load, store in zip(loads, stores):
        load.wait()
        store.start()
    for store in stores:
        store.wait()


def shards(queries, passages, positives, hard_ids):
    dma = pltpu.SemaphoreType.DMA
    any_spec = pl.BlockSpec(memory_space=pl.ANY)
    vmem_spec = pl.BlockSpec(memory_space=pltpu.VMEM)
    query_grads, passage_grads, losses = pl.pallas_call(
        kernel,
        out_shape=(
            jax.ShapeDtypeStruct((Q, D), BF16),
            jax.ShapeDtypeStruct((PB, D), BF16),
            jax.ShapeDtypeStruct((Q // 128, 128), F32),
        ),
        in_specs=[any_spec, any_spec, vmem_spec, vmem_spec],
        out_specs=(any_spec, vmem_spec, vmem_spec),
        scratch_shapes=[
            pltpu.VMEM((PB, D), BF16),
            pltpu.VMEM((Q, D), BF16),
            pltpu.VMEM((Q, D), BF16),
            pltpu.VMEM((4 * CH, D), BF16),
            pltpu.VMEM((4 * SL, D), BF16),
            pltpu.VMEM((4 * SL, D), BF16),
            pltpu.VMEM((4 * SL, D), BF16),
            pltpu.VMEM((4 * CH, D), BF16),
            pltpu.VMEM((4 * SL, D), BF16),
            pltpu.VMEM((SL, D), BF16),
            pltpu.VMEM((SL, D), BF16),
            pltpu.VMEM((SL, D), BF16),
            pltpu.VMEM((PB, D), BF16),
            pltpu.VMEM((Q, 4 * CH), F32),
            pltpu.VMEM((Q, 4 * SL), F32),
            pltpu.VMEM((Q, 4 * CH), BF16),
            pltpu.VMEM((4 * CH, Q), BF16),
            pltpu.VMEM((Q, 4 * SL), BF16),
            pltpu.VMEM((4 * SL, Q), BF16),
            pltpu.VMEM((256, D), F32),
            pltpu.VMEM((4 * SL, CH), BF16),
            pltpu.VMEM((4 * CH, SL), BF16),
            pltpu.VMEM((8, 8, 128), F32),
            pltpu.VMEM((Q, 128), F32),
            pltpu.VMEM((Q, 128), jnp.int32),
            pltpu.VMEM((Q, 1), jnp.int32),
            dma((8,)),
            dma((15 * PARTS,)), dma((15 * PARTS,)),
            dma((8,)), dma((8,)),
            dma((STEPS, 8)), dma((STEPS, 8)),
            dma((STEPS, 8)), dma((STEPS, 8)),
            dma((10 * PARTS,)), dma((10 * PARTS,)),
        ],
        compiler_params=pltpu.CompilerParams(
            collective_id=0, has_side_effects=True, vmem_limit_bytes=63 * 2**20
        ),
        cost_estimate=pl.CostEstimate(
            flops=6 * Q * 1536 * D, bytes_accessed=4 * Q * D, transcendentals=Q * 1536
        ),
    )(passages, queries, hard_ids.T, positives.reshape(1, Q))
    query_grads, passage_grads, losses = pl.pallas_call(
        hand_over,
        out_shape=(
            jax.ShapeDtypeStruct((Q, D), BF16),
            jax.ShapeDtypeStruct((PB, D), BF16),
            jax.ShapeDtypeStruct((Q // 128, 128), F32),
        ),
        in_specs=[any_spec] * 3,
        out_specs=(any_spec,) * 3,
        scratch_shapes=[
            pltpu.VMEM((Q, D), BF16),
            pltpu.VMEM((PB, D), BF16),
            pltpu.VMEM((Q // 128, 128), F32),
            dma((10,)),
            dma((10,)),
        ],
        compiler_params=pltpu.CompilerParams(vmem_limit_bytes=63 * 2**20),
        cost_estimate=pl.CostEstimate(flops=0, bytes_accessed=4 * Q * D, transcendentals=0),
    )(query_grads, passage_grads, losses)
    return query_grads, passage_grads, losses.reshape(Q)


def solution(mesh):
    in_specs = (
        P(("blk", "group"), None),
        P(("blk", "group"), None),
        P(("blk", "group")),
        P(("blk", "group"), None),
    )
    out_specs = (P(("blk", "group"), None), P(("blk", "group"), None), P(("blk", "group")))
    return jax.shard_map(shards, mesh=mesh, in_specs=in_specs, out_specs=out_specs, check_vma=False)
```

```python
import jax
import jax.numpy as jnp
from jax import lax
from jax.experimental import pallas as pl
from jax.experimental.pallas import tpu as pltpu
from jax.sharding import PartitionSpec as P

D = 4096
Q = 512
PB = 64
HARD = 8
CAP = 4
SCALE = 20.0
EPS = 1e-06
CH = 256
SL = 128
PARTS = 4
PW = D // PARTS
TN = 512
HALF = PARTS // 2
ALL_PARTS = tuple(range(PARTS))
AHEAD = (4,) * 16
STEPS = 4 * PARTS
BWD_STEPS = tuple((j, cq) for j in (3, 2, 1, 0) for cq in ALL_PARTS)
MESH = pl.DeviceIdType.MESH
F32 = jnp.float32
BF16 = jnp.bfloat16
NT = (((1,), (1,)), ((), ()))
TN_DIMS = (((0,), (0,)), ((), ()))


def iota(shape, dim):
    return lax.broadcasted_iota(jnp.int32, shape, dim)


def inv_rel(rel):
    return ((4 - rel // 2) % 4) * 2 + rel % 2


def flips(rel):
    return (rel % 2) & (rel // 2 % 2)


def seen_by(rel, j):
    return (0, 2, 1, 3)[j] if flips(rel) else j


def dot(a, b):
    return jnp.dot(a, b, preferred_element_type=F32)


def onehot(mask):
    return jnp.where(mask, 1.0, 0.0).astype(BF16)


def kernel(
    passages, queries, ids_ref, pos_ref, out_q, out_p, out_l,
    pv, qv, qhat, hat, fsend, fetched, sret, part, sibr, z2, z1m, z1p, xr,
    exp_c, exp_h, wc, wct, wh, wht, qsum, sel, selt, tabs, qinv, key_ref, kk_ref,
    lsem, ag_s, ag_r, tab_s, tab_r, f_s, f_r, r_s, r_r, rs_s, rs_r,
):
    blk = lax.axis_index("blk")
    grp = lax.axis_index("group")
    xh, z, core = blk // 8, (blk // 2) % 4, blk % 2
    y, xl = grp // 2, grp % 2

    def dev(dxh=0, dz=0, dc=0, dy=0, dxl=0):
        return (
            ((xh + dxh) % 2) * 8 + ((z + dz) % 4) * 2 + (core + dc) % 2,
            ((y + dy) % 4) * 2 + (xl + dxl) % 2,
        )

    sib, zp, zm, xo = dev(dc=1), dev(dz=1), dev(dz=3), dev(dxh=1)
    partner = [
        dev(dy=rel // 2, dxl=rel % 2, dxh=flips(rel)) for rel in range(8)
    ]

    barrier = pltpu.get_barrier_semaphore()
    for d in [sib, zp, zm, xo] + partner[1:]:
        pl.semaphore_signal(barrier, inc=1, device_id=d, device_id_type=MESH)

    load_p = pltpu.make_async_copy(passages, pv, lsem.at[0])
    load_q = pltpu.make_async_copy(queries, qv, lsem.at[1])
    load_p.start()
    load_q.start()

    def remote(src, dst, ss, rs, d):
        return pltpu.make_async_remote_copy(
            src_ref=src, dst_ref=dst, send_sem=ss, recv_sem=rs, device_id=d, device_id_type=MESH
        )

    def cols(part_id):
        return pl.ds(part_id * PW, PW)

    ag = {}

    def row(dz, dc, dxh):
        chunk, side = (1 + dxh, dz // 2) if dz % 2 else (dz // 2 * 3, dxh)
        return chunk * CH + dc * 2 * PB + side * PB

    def add_ag(name, src, dst, d, parts=ALL_PARTS):
        for cq in parts:
            i = len(ag)
            ag[name, cq] = remote(
                hat.at[pl.ds(src, PB), cols(cq)], hat.at[pl.ds(dst, PB), cols(cq)],
                ag_s.at[i], ag_r.at[i], d,
            )

    own = row(0, 0, 0)
    add_ag("x", own, row(0, 0, 1), xo)
    add_ag("m0", own, row(3, 0, 0), zp)
    add_ag("p0", own, row(1, 0, 0), zm)
    add_ag("s00", own, row(0, 1, 0), sib)
    add_ag("s01", row(0, 0, 1), row(0, 1, 1), sib)
    add_ag("m1", row(0, 0, 1), row(3, 0, 1), zp)
    add_ag("p1", row(0, 0, 1), row(1, 0, 1), zm)
    for dxh in range(2):
        add_ag(f"s3{dxh}", row(3, 0, dxh), row(3, 1, dxh), sib)
        add_ag(f"s1{dxh}", row(1, 0, dxh), row(1, 1, dxh), sib)
        add_ag(f"t{dxh}", row(3, 0, dxh), row(2, 0, dxh), zp, ALL_PARTS[:HALF])
        add_ag(f"t{dxh}", row(1, 0, dxh), row(2, 0, dxh), zm, ALL_PARTS[HALF:])
        add_ag(f"s2{dxh}", row(2, 0, dxh), row(2, 1, dxh), sib)

    fetch, back = {}, {}
    for step, (j, cq) in enumerate(BWD_STEPS):
        for rel in range(1, 8):
            to, theirs = inv_rel(rel), seen_by(rel, j)
            fetch[j, cq, rel] = remote(
                fsend.at[pl.ds(j * SL + rel * 16, 16), cols(cq)],
                fetched.at[pl.ds(theirs * SL + to * 16, 16), cols(cq)],
                f_s.at[step, rel], f_r.at[step, to], partner[rel],
            )
            back[j, cq, rel] = remote(
                fsend.at[pl.ds(theirs * SL + rel * 16, 16), cols(cq)],
                sret.at[pl.ds(j * SL + to * 16, 16), cols(cq)],
                r_s.at[step, rel], r_r.at[step, to], partner[rel],
            )

    rs = {}

    def add_rs(name, src, dst, d):
        i = len(rs)
        rs[name] = remote(src, dst, rs_s.at[i], rs_r.at[i], d)

    for j, cq in BWD_STEPS:
        add_rs(
            ("sib", j, cq),
            part.at[pl.ds(j * CH + SL, SL), cols(cq)], sibr.at[pl.ds(j * SL, SL), cols(cq)], sib,
        )
    for cq in ALL_PARTS:
        add_rs(
            ("z", 3, cq),
            part.at[pl.ds(3 * CH, SL), cols(cq)], z2.at[:, cols(cq)], zp if cq < HALF else zm,
        )
        for j in (2, 1):
            there = pl.ds((j - 1) * PB, PB)
            add_rs(
                ("zp", j, cq), part.at[pl.ds(j * CH, PB), cols(cq)], z1m.at[there, cols(cq)], zp
            )
            add_rs(
                ("zm", j, cq), part.at[pl.ds(j * CH + PB, PB), cols(cq)], z1p.at[there, cols(cq)], zm
            )
        add_rs(("x", cq), part.at[pl.ds(PB, PB), cols(cq)], xr.at[:, cols(cq)], xo)

    def place(block):
        dz = (lax.shift_right_logical(block, 1) - z) & 3
        dxh = lax.shift_right_logical(block, 3) ^ xh
        odd, far = (dz & 1) == 1, lax.shift_right_logical(dz, 1)
        chunk, side = jnp.where(odd, 1 + dxh, 3 * far), jnp.where(odd, far, dxh)
        return chunk, ((block & 1) ^ core) * 2 + side

    ids = ids_ref[...]
    owner = lax.shift_right_logical(ids, 6)
    og = owner & 7
    rel_g = ((lax.shift_right_logical(og, 1) - y) & 3) * 2 + ((og & 1) ^ xl)
    chunk, o = place(lax.shift_right_logical(owner, 3))
    keys = (rel_g * 16 + chunk * 4 + o) * 64 + (ids & 63)
    count = jnp.zeros((128, 128), F32)
    sub_q = iota((128, Q), 0)
    for h in range(HARD):
        key = keys[h : h + 1]
        hi = onehot(lax.shift_right_logical(key, 6) == sub_q)
        lo = onehot((key & 63) == sub_q)
        count = count + lax.dot_general(lo, hi, NT, preferred_element_type=F32)
    present = count > 0.5
    sub = iota((128, 128), 0)
    rank = dot(onehot(iota((128, 128), 1) < sub), onehot(present))
    table = jnp.zeros((8, 128), F32)
    for slot in range(CAP):
        hit = jnp.where(
            jnp.logical_and(present, rank == float(slot)), (sub + 1).astype(F32), 0.0
        )
        found = jnp.sum(hit, axis=0, keepdims=True) - 1.0
        table = jnp.where(iota((8, 128), 0) == slot, found, table)
    tabs[0] = table

    load_p.wait()
    raw = pv[...].astype(F32)
    pinv = 1.0 / jnp.sqrt(jnp.sum(raw * raw, axis=1, keepdims=True) + EPS)
    hat[pl.ds(own, PB), :] = (raw * pinv).astype(BF16)
    pl.semaphore_wait(barrier, 11)

    def own_send(cq):
        for name in ("x", "m0", "p0", "s00"):
            if cq >= 2:
                ag[name, cq - 2].wait_send()
                gone.add((name, cq - 2))
            ag[name, cq].start()

    gone = set()
    own_send(0)

    ask = []
    for rel in range(1, 8):
        to = inv_rel(rel)
        ask.append(remote(tabs.at[0], tabs.at[to], tab_s.at[rel], tab_r.at[to], partner[rel]))
        ask[-1].start()

    load_q.wait()

    def norm_rows(i, carry):
        rows = pl.ds(pl.multiple_of(i * 32, 32), 32)
        values = qv[rows, :].astype(F32)
        inverse = 1.0 / jnp.sqrt(jnp.sum(values * values, axis=1, keepdims=True) + EPS)
        qinv[rows, :] = jnp.broadcast_to(inverse, (32, 128))
        qhat[rows, :] = (values * inverse).astype(BF16)
        return carry

    def norm_queries(first, last):
        lax.fori_loop(first, last, norm_rows, 0)

    def build_selection():
        everything = tabs[...].reshape(64, 128).astype(BF16)
        lane = iota((128, 128), 1)
        who, o, slot = lane >> 4, (lane >> 2) & 3, lane & 3
        back_rel = ((4 - (who >> 1)) & 3) * 2 + (who & 1)
        flip = (who & 1) & ((who >> 1) & 1)
        diag = iota((64, 128), 0) == (who * 8 + slot)[:64]
        for j in range(4):
            theirs = jnp.where(flip == 1, (0, 2, 1, 3)[j], j)
            offset = (o >> 1) * 128 + ((o & 1) ^ (flip if j in (0, 3) else 0)) * 64
            pick = onehot(iota((128, 128), 0) == back_rel * 16 + theirs * 4 + o)
            local = jnp.sum(jnp.where(diag, dot(everything, pick), 0.0), axis=0, keepdims=True)
            target = jnp.where(local >= 0.0, local + offset[:1].astype(F32), -1.0)
            match = jnp.where(iota((CH, SL), 0).astype(F32) == target, 1.0, 0.0)
            selt[pl.ds(j * CH, CH), :] = match.astype(BF16)
            sel[pl.ds(j * SL, SL), :] = jnp.transpose(match).astype(BF16)

    def build_mask():
        lane = iota((128, Q), 1)
        from_lane = ((lane >> 4) & 7) * 16 + (lane >> 7) * 4 + ((lane >> 2) & 3)
        spread = dot(table.astype(BF16), onehot(iota((128, Q), 0) == from_lane))
        local = jnp.sum(
            jnp.where(iota((8, Q), 0) == (lane & 3)[:8], spread, 0.0), axis=0, keepdims=True
        )
        wanted = jnp.where(local >= 0.0, from_lane[:1] * 64 + local.astype(jnp.int32), -1)

        def rows_mask(i, carry):
            rows = pl.ds(pl.multiple_of(i * 64, 64), 64)
            mine = key_ref[rows, :]
            found = mine[:, 0:1] == wanted
            for h in range(1, HARD):
                found = jnp.logical_or(found, mine[:, h : h + 1] == wanted)
            exp_h[rows, :] = jnp.where(found, 1.0, 0.0)
            return carry

        lax.fori_loop(0, Q // 64, rows_mask, 0)

    def select(j, cq):
        def tile(n, carry):
            at = pl.ds(pl.multiple_of(cq * PW + n * TN, TN), TN)
            rows = dot(sel[pl.ds(j * SL, SL), :], hat[pl.ds(j * CH, CH), at]).astype(BF16)
            fsend[pl.ds(j * SL, SL), at] = rows
            fetched[pl.ds(j * SL, 16), at] = rows[:16]
            return carry

        lax.fori_loop(0, PW // TN, tile, 0)
        for rel in range(1, 8):
            fetch[j, cq, rel].start()

    totals = {"cycle": jnp.zeros((Q, 1), F32), "pos": jnp.zeros((Q, 1), F32)}

    def cycle_scores(j):
        scores = SCALE * lax.dot_general(
            qhat[...], hat[pl.ds(j * CH, CH), :], NT, preferred_element_type=F32
        )
        raised = jnp.exp(scores)
        exp_c[:, pl.ds(j * CH, CH)] = raised
        positive = kk_ref[...] == iota((Q, CH), 1) + j * CH
        totals["cycle"] = totals["cycle"] + jnp.sum(raised, axis=1, keepdims=True)
        totals["pos"] = totals["pos"] + jnp.sum(
            jnp.where(positive, scores, 0.0), axis=1, keepdims=True
        )

    positives = pos_ref[...]
    chunk, o = place(lax.shift_right_logical(positives, 6))
    spots = chunk * CH + o * PB + (positives & 63)
    stacked = jnp.concatenate(
        [keys.astype(F32), jnp.broadcast_to(spots.astype(F32), (120, Q))], axis=0
    )
    turned = jnp.transpose(stacked).astype(jnp.int32)
    key_ref[...] = turned
    kk_ref[...] = turned[:, HARD : HARD + 1]

    def sib_relay(cq, *names):
        for came, sent in names:
            ag[came, cq].wait_recv()
            ag[sent, cq].start()

    def z_relay(dxh, cq):
        ag[f"t{dxh}", cq].start()

    def from_sib(cq, *names):
        for name in names:
            ag[name, cq].wait_recv()

    own_send(1)
    norm_queries(0, 4)
    own_send(2)
    for copy in ask:
        copy.wait_recv()
    build_selection()
    own_send(3)
    for cq in ALL_PARTS:
        sib_relay(cq, ("x", "s01"), ("m0", "s30"), ("p0", "s10"))
        ag["m1", cq].start()
        ag["p1", cq].start()
        z_relay(0, cq)
        norm_queries(4 + 3 * cq, 7 + 3 * cq)
        from_sib(cq, "s00", "s01")
        select(0, cq)
        from_sib(cq, "s30", "s10")
        select(1, cq)
    for cq in ALL_PARTS:
        sib_relay(cq, ("m1", "s31"), ("p1", "s11"))
        z_relay(1, cq)
        from_sib(cq, "s31", "s11")
        select(2, cq)
    for j in range(3):
        cycle_scores(j)
    for cq in ALL_PARTS:
        sib_relay(cq, ("t0", "s20"), ("t1", "s21"))
    for cq in ALL_PARTS:
        from_sib(cq, "s20", "s21")
        select(3, cq)
    cycle_scores(3)
    build_mask()

    pos_score = totals["pos"]
    pos_exp = jnp.exp(pos_score)
    hard_total = pos_exp
    for (j, cq, rel), copy in fetch.items():
        if j != 3:
            copy.wait_send()
    for step in ((0, 1, 2), (3,)):
        at = pl.ds(step[0] * SL, len(step) * SL)
        scores = jnp.zeros((Q, len(step) * SL), F32)
        for piece in (ALL_PARTS,) if step[0] == 0 else [(cq,) for cq in ALL_PARTS]:
            for j in step:
                for cq in piece:
                    for rel in range(1, 8):
                        fetch[j, cq, rel].wait_recv()
            here = pl.ds(piece[0] * PW, len(piece) * PW)
            scores = scores + SCALE * lax.dot_general(
                qhat[:, here], fetched[at, here], NT, preferred_element_type=F32
            )
        raised = exp_h[:, at] * jnp.exp(scores)
        exp_h[:, at] = raised
        hard_total = hard_total + jnp.sum(raised, axis=1, keepdims=True)
    for (j, cq, rel), copy in fetch.items():
        if j == 3:
            copy.wait_send()
    hard_inv = 1.0 / hard_total

    def back_sums(first, chunks, parts=ALL_PARTS):
        slots = pl.ds(first * SL, chunks * SL)

        def tile(n, carry):
            at = pl.ds(pl.multiple_of(n * TN, TN), TN)
            rows = (SCALE * dot(wht[slots, :], qhat[:, at])).astype(BF16)
            fsend[slots, at] = rows
            for i in range(chunks):
                sret[pl.ds((first + i) * SL, 16), at] = rows[i * SL : i * SL + 16]
            return carry

        lax.fori_loop(parts[0] * PW // TN, (parts[-1] + 1) * PW // TN, tile, 0)

    def hard_weights(first, chunks):
        slots = pl.ds(first * SL, chunks * SL)
        weights = exp_h[:, slots] * hard_inv
        wh[:, slots] = weights.astype(BF16)
        wht[slots, :] = jnp.transpose(weights).astype(BF16)

    left = set()

    def back_start(step):
        j, cq = BWD_STEPS[step]
        for rel in range(1, 8):
            earlier = BWD_STEPS[max(step - AHEAD[step], 0)] + (rel,)
            if step >= AHEAD[step] and earlier not in left:
                back[earlier].wait_send()
                left.add(earlier)
            back[j, cq, rel].start()

    hard_weights(3, 1)
    back_sums(3, 1, ALL_PARTS[:1])
    back_start(0)
    back_sums(3, 1, ALL_PARTS[1:])
    back_start(1)
    hard_weights(0, 3)
    back_sums(0, 3)
    for step in range(2, AHEAD[0]):
        back_start(step)

    cycle_total = totals["cycle"]
    losses = jnp.log(cycle_total) + jnp.log(hard_total) - 2.0 * pos_score
    for i in range(Q // 128):
        spread = jnp.broadcast_to(losses[i * 128 : (i + 1) * 128], (128, 128))
        out_l[pl.ds(i, 1), :] = jnp.transpose(spread)[:1]
    cycle_inv = 1.0 / cycle_total
    correction = 2.0 - pos_exp * hard_inv
    for j in (3, 2, 1, 0):
        at = pl.ds(j * CH, CH)
        positive = kk_ref[...] == iota((Q, CH), 1) + j * CH
        weights = exp_c[:, at] * cycle_inv - jnp.where(positive, correction, 0.0)
        wc[:, at] = weights.astype(BF16)
        wct[at, :] = jnp.transpose(weights).astype(BF16)

    QR = 256
    store_q = []
    along_q = {}

    def query_tiles(block, first, last):
        rows = pl.ds(block * QR, QR)
        inverse = qinv[rows, 0:1]

        def product(n, total):
            at = pl.ds(pl.multiple_of(n * TN, TN), TN)
            tile = SCALE * (dot(wc[rows, :], hat[:, at]) + dot(wh[rows, :], fetched[:, at]))
            qsum[:, at] = tile
            unit = qv[rows, at].astype(F32) * inverse
            return total + jnp.sum(unit * tile, axis=1, keepdims=True)

        start = along_q.get(block, jnp.zeros((QR, 1), F32))
        along_q[block] = lax.fori_loop(first, last, product, start)

    def query_store(block):
        rows = pl.ds(block * QR, QR)
        inverse = qinv[rows, 0:1]
        along = along_q[block]

        def project(n, carry):
            at = pl.ds(pl.multiple_of(n * TN, TN), TN)
            unit = qv[rows, at].astype(F32) * inverse
            qv[rows, at] = ((qsum[:, at] - unit * along) * inverse).astype(BF16)
            return carry

        lax.fori_loop(0, D // TN, project, 0)
        store_q.append(
            pltpu.make_async_copy(qv.at[rows, :], out_q.at[rows, :], lsem.at[2 + block])
        )
        store_q[-1].start()

    def query_work(i):
        block, piece = i // 3, i % 3
        if piece < 2:
            query_tiles(block, piece * 4, piece * 4 + 4)
        else:
            query_store(block)

    def partial(j, cq):
        def tile(n, carry):
            at = pl.ds(pl.multiple_of(cq * PW + n * TN, TN), TN)
            total = SCALE * dot(wct[pl.ds(j * CH, CH), :], qhat[:, at]) + dot(
                selt[pl.ds(j * CH, CH), :], sret[pl.ds(j * SL, SL), at]
            )
            part[pl.ds(j * CH, CH), at] = total.astype(BF16)
            return carry

        lax.fori_loop(0, PW // TN, tile, 0)
        rs["sib", j, cq].start()

    def reduce(j, cq):
        at = cols(cq)
        mine = pl.ds(j * CH, SL)
        rs["sib", j, cq].wait_recv()
        total = part[mine, at].astype(F32) + sibr[pl.ds(j * SL, SL), at].astype(F32)
        if j == 3:
            part[mine, at] = total.astype(BF16)
            rs["z", 3, cq].start()
        elif j > 0:
            here = pl.ds((j - 1) * PB, PB)
            rs["z", 3, cq].wait_recv() if j == 2 else None
            more = z2[here, at].astype(F32)
            first, second = total[:PB], total[PB:]
            if cq < HALF:
                first = first + more
            else:
                second = second + more
            part[pl.ds(j * CH, PB), at] = first.astype(BF16)
            rs["zp", j, cq].start()
            part[pl.ds(j * CH + PB, PB), at] = second.astype(BF16)
            rs["zm", j, cq].start()
        else:
            for dxh in (1, 0):
                rs["zp", 1 + dxh, cq].wait_recv()
                rs["zm", 1 + dxh, cq].wait_recv()
                here = pl.ds(dxh * PB, PB)
                both = z1m[here, at].astype(F32) + z1p[here, at].astype(F32)
                both = both + total[dxh * PB : (dxh + 1) * PB]
                if dxh == 1:
                    part[here, at] = both.astype(BF16)
                    rs["x", cq].start()
                else:
                    qsum[:PB, at] = both

    for key, copy in ag.items():
        if key not in gone:
            copy.wait_send()
    for copy in ask:
        copy.wait_send()
    for i in range(3):
        query_work(i)
    waiting, started = [], AHEAD[0]
    for step, (j, cq) in enumerate(BWD_STEPS):
        for rel in range(1, 8):
            back[j, cq, rel].wait_recv()
        while started < STEPS and started - AHEAD[started] <= step:
            back_start(started)
            started += 1
        partial(j, cq)
        waiting.append((j, cq))
        while len(waiting) > (1 if step < 12 else 0):
            reduce(*waiting.pop(0))
        if step in (3, 5, 7):
            query_work(3 + (step - 3) // 2)

    for key, copy in back.items():
        if key not in left:
            copy.wait_send()
    for key, copy in rs.items():
        if key[0] != "x":
            copy.wait_send()
    for copy in store_q:
        copy.wait()
    unit = pv[...].astype(F32) * pinv
    for cq in ALL_PARTS:
        rs["x", cq].wait_recv()
    total = qsum[:PB, :] + xr[...].astype(F32)
    along = jnp.sum(unit * total, axis=1, keepdims=True)
    out_p[...] = ((total - unit * along) * pinv).astype(BF16)

    for cq in ALL_PARTS:
        rs["x", cq].wait_send()


def hand_over(in_q, in_p, in_l, out_q, out_p, out_l, hold_q, hold_p, hold_l, sem_in, sem_out):
    pieces = [(in_p, hold_p, out_p), (in_l, hold_l, out_l)]
    for i in range(8):
        rows = pl.ds(i * (Q // 8), Q // 8)
        pieces.append((in_q.at[rows, :], hold_q.at[rows, :], out_q.at[rows, :]))
    loads, stores = [], []
    for i, (source, hold, target) in enumerate(pieces):
        loads.append(pltpu.make_async_copy(source, hold, sem_in.at[i]))
        stores.append(pltpu.make_async_copy(hold, target, sem_out.at[i]))
    for load in loads:
        load.start()
    for load, store in zip(loads, stores):
        load.wait()
        store.start()
    for store in stores:
        store.wait()


def shards(queries, passages, positives, hard_ids):
    dma = pltpu.SemaphoreType.DMA
    any_spec = pl.BlockSpec(memory_space=pl.ANY)
    vmem_spec = pl.BlockSpec(memory_space=pltpu.VMEM)
    query_grads, passage_grads, losses = pl.pallas_call(
        kernel,
        out_shape=(
            jax.ShapeDtypeStruct((Q, D), BF16),
            jax.ShapeDtypeStruct((PB, D), BF16),
            jax.ShapeDtypeStruct((Q // 128, 128), F32),
        ),
        in_specs=[any_spec, any_spec, vmem_spec, vmem_spec],
        out_specs=(any_spec, vmem_spec, vmem_spec),
        scratch_shapes=[
            pltpu.VMEM((PB, D), BF16),
            pltpu.VMEM((Q, D), BF16),
            pltpu.VMEM((Q, D), BF16),
            pltpu.VMEM((4 * CH, D), BF16),
            pltpu.VMEM((4 * SL, D), BF16),
            pltpu.VMEM((4 * SL, D), BF16),
            pltpu.VMEM((4 * SL, D), BF16),
            pltpu.VMEM((4 * CH, D), BF16),
            pltpu.VMEM((4 * SL, D), BF16),
            pltpu.VMEM((SL, D), BF16),
            pltpu.VMEM((SL, D), BF16),
            pltpu.VMEM((SL, D), BF16),
            pltpu.VMEM((PB, D), BF16),
            pltpu.VMEM((Q, 4 * CH), F32),
            pltpu.VMEM((Q, 4 * SL), F32),
            pltpu.VMEM((Q, 4 * CH), BF16),
            pltpu.VMEM((4 * CH, Q), BF16),
            pltpu.VMEM((Q, 4 * SL), BF16),
            pltpu.VMEM((4 * SL, Q), BF16),
            pltpu.VMEM((256, D), F32),
            pltpu.VMEM((4 * SL, CH), BF16),
            pltpu.VMEM((4 * CH, SL), BF16),
            pltpu.VMEM((8, 8, 128), F32),
            pltpu.VMEM((Q, 128), F32),
            pltpu.VMEM((Q, 128), jnp.int32),
            pltpu.VMEM((Q, 1), jnp.int32),
            dma((8,)),
            dma((15 * PARTS,)), dma((15 * PARTS,)),
            dma((8,)), dma((8,)),
            dma((STEPS, 8)), dma((STEPS, 8)),
            dma((STEPS, 8)), dma((STEPS, 8)),
            dma((10 * PARTS,)), dma((10 * PARTS,)),
        ],
        compiler_params=pltpu.CompilerParams(
            collective_id=0, has_side_effects=True, vmem_limit_bytes=63 * 2**20
        ),
        cost_estimate=pl.CostEstimate(
            flops=6 * Q * 1536 * D, bytes_accessed=4 * Q * D, transcendentals=Q * 1536
        ),
    )(passages, queries, hard_ids.T, positives.reshape(1, Q))
    query_grads, passage_grads, losses = pl.pallas_call(
        hand_over,
        out_shape=(
            jax.ShapeDtypeStruct((Q, D), BF16),
            jax.ShapeDtypeStruct((PB, D), BF16),
            jax.ShapeDtypeStruct((Q // 128, 128), F32),
        ),
        in_specs=[any_spec] * 3,
        out_specs=(any_spec,) * 3,
        scratch_shapes=[
            pltpu.VMEM((Q, D), BF16),
            pltpu.VMEM((PB, D), BF16),
            pltpu.VMEM((Q // 128, 128), F32),
            dma((10,)),
            dma((10,)),
        ],
        compiler_params=pltpu.CompilerParams(vmem_limit_bytes=63 * 2**20),
        cost_estimate=pl.CostEstimate(flops=0, bytes_accessed=4 * Q * D, transcendentals=0),
    )(query_grads, passage_grads, losses)
    return query_grads, passage_grads, losses.reshape(Q)


def solution(mesh):
    in_specs = (
        P(("blk", "group"), None),
        P(("blk", "group"), None),
        P(("blk", "group")),
        P(("blk", "group"), None),
    )
    out_specs = (P(("blk", "group"), None), P(("blk", "group"), None), P(("blk", "group")))
    return jax.shard_map(shards, mesh=mesh, in_specs=in_specs, out_specs=out_specs, check_vma=False)
```
